128 devices in a mesh: gx: 8 (over z, y_hi), bulk: 16 (over y_lo, x, core).
Axes of the slice: x: 4, y: 4 (y_hi: 2, y_lo: 2; y = y_hi * 2 + y_lo), z: 4, core: 2. Of those that a mesh axis runs over, the one named last changes fastest.
Arguments:
- saved_thermal_state: float32 [256, 512, 256], P('gx', 'bulk'), may hold values from -6 to 6
- thermal_diffusivity: float32 [256, 512, 256], P('gx', 'bulk'), may hold values from 0.25 to 1
- patch_power_density: float32 [1048576], P(('gx', 'bulk')), may hold values from -6 to 6
- entry_position: int32 [256, 512], P('gx', 'bulk'), may hold values from 0 to 1023
- incoming_patch_table: int32 [128, 128, 8], P(('gx', 'bulk')), may hold values from 0 to 8191
- terminal_sensitivity: float32 [256, 512, 256], P('gx', 'bulk'), may hold values from -6 to 6
Outputs:
- flux_grad: float32 [1048576], P(('gx', 'bulk'))
- start_adjoint: float32 [256, 512, 256], P('gx', 'bulk')
The draws below stay inside these ranges and needn't reach their ends.
All inputs are finite; a program needn't handle non-finite values.
Results may differ from the reference program's by a relative error of at most 0.00002.
Values sent between devices are 32-bit elements; how exact they have to be, the bound alone decides.
A program may use at most 320 MiB of HBM per device.

```python
import jax
import jax.numpy as jnp

CX = 32
CY = 32
VERTICAL_CELLS = 256
STEPS = 3
CAP = 8
PD = 8192
LENGTHWISE_CELLS = 256
TRANSVERSE_CELLS = 512
PATCHES = 1048576
N_BULK = 16
DEVICES = 128


def plant(entries, own_key, least, largest):
    extent = entries.shape
    spot = [jax.random.randint(jax.random.fold_in(own_key, axis), (), 0, extent[axis]) for axis in range(len(extent))]
    entries = entries.at[tuple(spot)].set(least)
    longest = extent.index(max(extent))
    spot[longest] = (spot[longest] + 1) % extent[longest]
    return entries.at[tuple(spot)].set(largest)


def block_levels(stream_key, shape, pieces, smallest, high):
    factor_of = 1.0
    for dim, parts in pieces:
        steps = jax.random.uniform(jax.random.fold_in(jax.random.fold_in(stream_key, 6), dim), (parts,), jnp.float32, smallest / len(pieces), high / len(pieces))
        factor_of = factor_of * jnp.repeat(jnp.exp(steps), shape[dim] // parts).reshape((-1,) + (1,) * (len(shape) - 1 - dim))
    return factor_of


def scatter_about(stream_key, dims, scale, limit, cuts=(), kind=jnp.bfloat16):
    gain = block_levels(stream_key, dims, cuts, -0.22, 0.18) if cuts else 1.0
    drawn = jax.random.normal(stream_key, dims, jnp.float32) * scale * gain
    return jnp.minimum(jnp.maximum(drawn, -limit), limit).astype(kind)


def setup_inputs(seed: int = 0) -> dict:
    key_of = jax.random.split(jax.random.key(seed), 7)
    return {
        "saved_thermal_state": scatter_about(key_of[0], (LENGTHWISE_CELLS, TRANSVERSE_CELLS, VERTICAL_CELLS), 1.0, 6.0, ((0, 8), (1, 16)), jnp.float32),
        "thermal_diffusivity": jnp.clip(0.25 + 0.75 * jax.random.uniform(key_of[1], (LENGTHWISE_CELLS, TRANSVERSE_CELLS, VERTICAL_CELLS), jnp.float32) ** block_levels(key_of[1], (LENGTHWISE_CELLS, TRANSVERSE_CELLS, VERTICAL_CELLS), ((0, 8), (1, 16)), -0.2, 0.2), 0.25, 1.0),
        "patch_power_density": scatter_about(key_of[2], (PATCHES,), 1.0, 6.0, ((0, 128),), jnp.float32),
        "entry_position": plant(jax.random.randint(key_of[3], (LENGTHWISE_CELLS, TRANSVERSE_CELLS), 0, DEVICES * CAP), jax.random.fold_in(key_of[3], 1), 0, (DEVICES * CAP) - 1).astype(jnp.int32),
        "incoming_patch_table": plant(jax.random.randint(key_of[4], (DEVICES, DEVICES, CAP), 0, PD), jax.random.fold_in(key_of[4], 1), 0, PD - 1).astype(jnp.int32),
        "terminal_sensitivity": scatter_about(key_of[5], (LENGTHWISE_CELLS, TRANSVERSE_CELLS, VERTICAL_CELLS), 1.0, 6.0, ((0, 8), (1, 16)), jnp.float32),
    }


RATE = 0.08
DRIFT_VELOCITY = 0.2
SOURCE = 0.5

def boundary_plane_taker(padded, axis_number, start, stop):
    index_list = [slice(1, -1), slice(1, -1), slice(1, -1)]
    index_list[axis_number] = slice(start, stop)
    return padded[tuple(index_list)]

def integrate_onward(thermal_state, diffusion_bordered, thermal_input):
    thermal_bordered = jnp.pad(thermal_state, 1)
    diffusivity_bordered = diffusion_bordered * (1.0 + 0.5 * jnp.tanh(thermal_bordered))
    increment_result = thermal_state - DRIFT_VELOCITY * (thermal_state - boundary_plane_taker(thermal_bordered, 0, 0, -2))
    for axis_number in range(3):
        interface_diffusivity = 0.5 * (boundary_plane_taker(diffusivity_bordered, axis_number, 0, -1) + boundary_plane_taker(diffusivity_bordered, axis_number, 1, None))
        interface_transport = interface_diffusivity * (boundary_plane_taker(thermal_bordered, axis_number, 1, None) - boundary_plane_taker(thermal_bordered, axis_number, 0, -1))
        size_here = interface_transport.shape[axis_number]
        right_face = lax_slice(interface_transport, axis_number, 1, size_here)
        left_face = lax_slice(interface_transport, axis_number, 0, size_here - 1)
        increment_result = increment_result + RATE * (right_face - left_face)
    return increment_result.at[:, :, 0].add(SOURCE * thermal_input)

def lax_slice(array, axis_number, start, stop):
    index_list = [slice(None), slice(None), slice(None)]
    index_list[axis_number] = slice(start, stop)
    return array[tuple(index_list)]

def reference(saved_thermal_state, thermal_diffusivity, patch_power_density, entry_position, incoming_patch_table, terminal_sensitivity):
    row_dev = jnp.arange(LENGTHWISE_CELLS, dtype=jnp.int32) // CX
    col_dev = jnp.arange(TRANSVERSE_CELLS, dtype=jnp.int32) // CY
    device = row_dev[:, None] * N_BULK + col_dev[None, :]
    owner = entry_position // CAP
    position = entry_position % CAP
    patch = owner * PD + incoming_patch_table[device, owner, position]
    diffusion_bordered = jnp.pad(thermal_diffusivity, 1)

    def iterate_increments(thermal_state, thermal_inflows):
        thermal_input = thermal_inflows[patch]
        for step_index in range(STEPS):
            thermal_state = integrate_onward(thermal_state, diffusion_bordered, thermal_input)
        return thermal_state
    terminal_thermal_state, vector_jacobian = jax.vjp(iterate_increments, saved_thermal_state, patch_power_density)
    start_adjoint, flux_grad = vector_jacobian(terminal_sensitivity)
    return (flux_grad, start_adjoint)
```

```python
import jax
import jax.numpy as jnp
from jax import lax
from jax.experimental import pallas as pl
from jax.experimental.pallas import tpu as pltpu
from jax.sharding import PartitionSpec as P

MESH = pl.DeviceIdType.MESH
RATE = 0.08
DRIFT = 0.2
SOURCE = 0.5
HALF_RATE = 0.5 * RATE

NG, NB = 8, 16
CX, CY, CZ = 32, 32, 256

T0, DD, L3, T1, T2, L2, L1 = range(7)


def split3(x):
    hi = x.astype(jnp.bfloat16)
    rest = x - hi.astype(jnp.float32)
    mid = rest.astype(jnp.bfloat16)
    low = (rest - mid.astype(jnp.float32)).astype(jnp.bfloat16)
    return hi, mid, low


def iota(shape, axis):
    return lax.broadcasted_iota(jnp.int32, shape, axis)


def kernel(
    t0_hbm, d_hbm, l3_hbm, patch_ref, entry_ref, table_ref,
    flux_ref, adj_ref,
    fld, kay, slp, yrecv, ysend, kyh, rows, gath, hot_e, hot_p,
    load_sem, xs_sem, xr_sem, g_send, g_recv, b_send, b_recv,
):
    g = lax.axis_index("gx")
    b = lax.axis_index("bulk")

    loads = [
        pltpu.make_async_copy(src, fld.at[f, pl.ds(1, CX)], load_sem.at[f])
        for f, src in ((T0, t0_hbm), (DD, d_hbm), (L3, l3_hbm))
    ]
    for load in loads:
        load.start()
    barrier = pltpu.get_barrier_semaphore()
    for k in range(1, NG):
        pl.semaphore_signal(barrier, inc=1, device_id=(lax.rem(g + k, NG), b), device_id_type=MESH)
    for k in range(1, NB):
        pl.semaphore_signal(barrier, inc=1, device_id=(g, lax.rem(b + k, NB)), device_id_type=MESH)

    lane = iota((8, 128), 1)
    sub = iota((8, 128), 0)

    def stage_one(n, block):
        for o in range(NG):
            rows[n, 0, o] = block[o:o + 1, :]
        copies = []
        for k in range(1, NG):
            o = lax.rem(g + k, NG)
            c = pltpu.make_async_remote_copy(
                src_ref=rows.at[n, 0, o], dst_ref=rows.at[n, 1, g],
                send_sem=g_send.at[n, k], recv_sem=g_recv.at[n, k],
                device_id=(o, b), device_id_type=MESH)
            c.start()
            copies.append(c)
        rows[n, 1, g] = rows[n, 0, g]
        return copies

    def stage_two(n, first):
        for c in first:
            c.wait_recv()
        gath[n, b] = jnp.concatenate([rows[n, 1, o] for o in range(NG)], axis=0)
        copies = []
        for k in range(1, NB):
            c = pltpu.make_async_remote_copy(
                src_ref=gath.at[n, b], dst_ref=gath.at[n, b],
                send_sem=b_send.at[n, k], recv_sem=b_recv.at[n, k],
                device_id=(g, lax.rem(b + k, NB)), device_id_type=MESH)
            c.start()
            copies.append(c)
        return copies

    def finish(n, second):
        for c in second:
            c.wait_recv()
        out = jnp.zeros((8, 128), jnp.float32)
        for s in range(NB):
            turned = pltpu.roll(gath[n, s], lax.rem(s - b + 128, 128), axis=1)
            out = out + jnp.where((lane & 15) == s, turned, 0.0)
        return out

    def make_hot(hot, low):
        for q in range(8):
            hit = iota((128, 128), 0) == low[q:q + 1, :]
            hot[:, q * 128:(q + 1) * 128] = jnp.where(hit, 1.0, 0.0).astype(jnp.bfloat16)

    def lookup(parts, hot, high, count):
        stacked = jnp.concatenate(parts, axis=0)
        found = jnp.dot(stacked, hot[...], preferred_element_type=jnp.float32)
        total = found[:count] + found[count:2 * count] + found[2 * count:]
        out = []
        for q in range(8):
            piece = total[:, q * 128:(q + 1) * 128]
            hit = iota((count, 128), 0) == high[q:q + 1, :]
            out.append(jnp.sum(jnp.where(hit, piece, 0.0), axis=0, keepdims=True))
        return jnp.concatenate(out, axis=0)

    def scatter(values, hot, high, count):
        spread = jnp.concatenate(
            [jnp.where(iota((count, 128), 0) == high[q:q + 1, :], values[q:q + 1, :], 0.0)
             for q in range(8)], axis=1)
        total = jnp.zeros((count, 128), jnp.float32)
        for part in split3(spread):
            total = total + lax.dot_general(
                part, hot[...], (((1,), (1,)), ((), ())), preferred_element_type=jnp.float32)
        return total

    table = table_ref[...].astype(jnp.float32)
    listed = jnp.zeros((8, 128), jnp.float32)
    for k in range(8):
        turned = pltpu.roll(table, 16 * k, axis=1) if k else table
        kept = jnp.where((lane >> 4) == sub, turned, 0.0)
        listed = listed + (pltpu.roll(kept, 8 - k, axis=0) if k else kept)

    def zero_edges():
        for edge, plane, side in ((g == 0, 0, None), (g == NG - 1, CX + 1, None),
                                  (b == 0, None, 0), (b == NB - 1, None, 1)):
            @pl.when(edge)
            def _():
                for f in range(7):
                    if plane is not None:
                        fld[f, plane] = jnp.zeros((CY, CZ), jnp.float32)
                    else:
                        yrecv[f, side] = jnp.zeros((CX, CZ), jnp.float32)

    def faces(f):
        def remote(src, dst, way, target):
            return pltpu.make_async_remote_copy(
                src_ref=src, dst_ref=dst, send_sem=xs_sem.at[f, way], recv_sem=xr_sem.at[f, way],
                device_id=target, device_id_type=MESH)
        return (
            (g > 0, g < NG - 1, remote(fld.at[f, 1], fld.at[f, CX + 1], 0, (lax.max(g - 1, 0), b))),
            (g < NG - 1, g > 0, remote(fld.at[f, CX], fld.at[f, 0], 1, (lax.min(g + 1, NG - 1), b))),
            (b > 0, b < NB - 1, remote(ysend.at[f, 0], yrecv.at[f, 1], 2, (g, lax.max(b - 1, 0)))),
            (b < NB - 1, b > 0, remote(ysend.at[f, 1], yrecv.at[f, 0], 3, (g, lax.min(b + 1, NB - 1)))),
        )

    def pack(f):
        def body(x, _):
            ysend[f, 0, pl.ds(x, 1), :] = fld[f, x + 1, 0:1, :]
            ysend[f, 1, pl.ds(x, 1), :] = fld[f, x + 1, CY - 1:CY, :]
            return 0
        lax.fori_loop(0, CX, body, 0)

    def send(f):
        for sends, _, c in faces(f):
            @pl.when(sends)
            def _():
                c.start()

    def arrive(f):
        for _, receives, c in faces(f):
            @pl.when(receives)
            def _():
                c.wait_recv()

    def sent(f):
        for sends, _, c in faces(f):
            @pl.when(sends)
            def _():
                c.wait_send()

    row = iota((CY, CZ), 0)
    col = iota((CY, CZ), 1)

    def y_low(a, edge):
        return jnp.where(row == 0, edge, pltpu.roll(a, 1, axis=0))

    def y_high(a, edge):
        return jnp.where(row == CY - 1, edge, pltpu.roll(a, CY - 1, axis=0))

    def k_low(a):
        return jnp.where(col == 0, 0.0, pltpu.roll(a, 1, axis=1))

    def k_high(a, edge):
        return jnp.where(col == CZ - 1, edge, pltpu.roll(a, CZ - 1, axis=1))

    def conduct(n, f):
        def body(x, _):
            h = jnp.tanh(fld[f, x])
            d = fld[DD, x] * HALF_RATE
            kay[n, x] = d + (0.5 * d) * h
            slp[n, x] = (0.5 * d) * (1.0 - h * h)
            return 0
        lax.fori_loop(1, CX + 1, body, 0)

    def conduct_halo(n, f):
        for x in (0, CX + 1):
            kay[n, x] = HALF_RATE * fld[DD, x] * (1.0 + 0.5 * jnp.tanh(fld[f, x]))
        for side in range(2):
            kyh[n, side] = HALF_RATE * yrecv[DD, side] * (1.0 + 0.5 * jnp.tanh(yrecv[f, side]))

    def forward(n, f, out):
        def body(x, flow_low):
            t, k = fld[f, x], kay[n, x]
            one = pl.ds(x - 1, 1)
            flow_high = (k + kay[n, x + 1]) * (fld[f, x + 1] - t)
            acc = (1.0 - DRIFT) * t + DRIFT * fld[f, x - 1] + (flow_high - flow_low)
            y_l = (k + y_low(k, kyh[n, 0, one, :])) * (t - y_low(t, yrecv[f, 0, one, :]))
            y_top = (k[CY - 1:CY] + kyh[n, 1, one, :]) * (yrecv[f, 1, one, :] - t[CY - 1:CY])
            acc = acc + (y_high(y_l, y_top) - y_l)
            k_l = (k + k_low(k)) * (t - k_low(t))
            acc = acc + (k_high(k_l, -(k * t)) - k_l)
            fld[out, x] = acc
            return flow_high
        first = (kay[n, 0] + kay[n, 1]) * (fld[f, 1] - fld[f, 0])
        lax.fori_loop(1, CX + 1, body, first)

    def reverse(n, f, lam, store):
        def body(x, carry):
            g_x, m_x = carry
            t, k, l = fld[f, x], kay[n, x], fld[lam, x]
            one = pl.ds(x - 1, 1)
            l_up = fld[lam, x + 1]
            w = l - l_up
            g_u = w * (fld[f, x + 1] - t)
            m_u = w * (k + kay[n, x + 1])
            bend = g_x + g_u
            acc = (1.0 - DRIFT) * l + DRIFT * l_up + (m_x - m_u)
            w = y_low(l, yrecv[lam, 0, one, :]) - l
            g_l = w * (t - y_low(t, yrecv[f, 0, one, :]))
            m_l = w * (k + y_low(k, kyh[n, 0, one, :]))
            last = slice(CY - 1, CY)
            w = l[last] - yrecv[lam, 1, one, :]
            g_t = w * (yrecv[f, 1, one, :] - t[last])
            m_t = w * (k[last] + kyh[n, 1, one, :])
            bend = bend + (g_l + y_high(g_l, g_t))
            acc = acc + (m_l - y_high(m_l, m_t))
            w = k_low(l) - l
            g_l = w * (t - k_low(t))
            m_l = w * (k + k_low(k))
            bend = bend + (g_l + k_high(g_l, -(l * t)))
            acc = acc + (m_l - k_high(m_l, l * k))
            store(x, acc + slp[n, x] * bend)
            return g_u, m_u
        w = fld[lam, 0] - fld[lam, 1]
        first = (w * (fld[f, 1] - fld[f, 0]), w * (kay[n, 0] + kay[n, 1]))
        lax.fori_loop(1, CX + 1, body, first)

    def into(f):
        def store(x, value):
            fld[f, x] = value
        return store

    def into_out(x, value):
        adj_ref[x - 1] = value

    def add_heat(f, columns):
        top = iota((CY, 128), 1) == 0
        for x in range(CX):
            c = columns[(x % 4) * CY:(x % 4 + 1) * CY, x // 4:x // 4 + 1]
            fld[f, x + 1, :, 0:128] = fld[f, x + 1, :, 0:128] + jnp.where(top, SOURCE * c, 0.0)

    def surface(f):
        wide = iota((128, 128), 1)
        total = jnp.zeros((128, 128), jnp.float32)
        for q in range(8):
            block = jnp.concatenate([fld[f, 4 * q + j + 1, :, 0:128] for j in range(4)], axis=0)
            total = total + jnp.where(wide == q, pltpu.roll(block, q, axis=1) if q else block, 0.0)
        return total.T[0:8, :]

    zero_edges()
    pl.semaphore_wait(barrier, NG - 1 + NB - 1)
    a_first = stage_one(0, listed)
    loads[0].wait()
    pack(T0)
    send(T0)
    loads[1].wait()
    pack(DD)
    send(DD)
    conduct(0, T0)
    a_second = stage_two(0, a_first)
    loads[2].wait()
    pack(L3)
    send(L3)

    entry = entry_ref[...]
    e_high = entry >> 7
    make_hot(hot_e, ((entry & 7) << 4) + ((entry >> 3) & 15))
    patches = split3(patch_ref[...])

    spot = finish(0, a_second).astype(jnp.int32)
    p_high = spot >> 7
    make_hot(hot_p, spot & 127)
    v_first = stage_one(1, lookup(patches, hot_p, p_high, 64))

    arrive(T0)
    arrive(DD)
    conduct_halo(0, T0)
    v_second = stage_two(1, v_first)
    forward(0, T0, T1)
    heat = lookup(split3(finish(1, v_second)), hot_e, e_high, 8)
    columns = jnp.transpose(heat)
    add_heat(T1, columns)
    pack(T1)
    send(T1)
    conduct(1, T1)
    arrive(T1)
    conduct_halo(1, T1)
    forward(1, T1, T2)
    add_heat(T2, columns)
    pack(T2)
    send(T2)
    conduct(2, T2)
    arrive(T2)
    conduct_halo(2, T2)
    arrive(L3)
    reverse(2, T2, L3, into(L2))
    pack(L2)
    send(L2)
    arrive(L2)
    reverse(1, T1, L2, into(L1))
    pack(L1)
    send(L1)
    total = surface(L3) + surface(L2) + surface(L1)
    slots = scatter(SOURCE * total, hot_e, e_high, 8)
    c_first = stage_one(2, slots)
    arrive(L1)
    c_second = stage_two(2, c_first)
    reverse(0, T0, L1, into_out)
    flux_ref[...] = scatter(finish(2, c_second), hot_p, p_high, 64)

    for copies in (a_first, a_second, v_first, v_second, c_first, c_second):
        for c in copies:
            c.wait_send()
    for f in range(7):
        sent(f)


def shards(state, diffusivity, patches, entries, table, sensitivity):
    anywhere = pl.BlockSpec(memory_space=pl.ANY)
    vmem = pl.BlockSpec(memory_space=pltpu.VMEM)
    f32, bf16 = jnp.float32, jnp.bfloat16
    flux, adjoint = pl.pallas_call(
        kernel,
        out_shape=(
            jax.ShapeDtypeStruct((64, 128), f32),
            jax.ShapeDtypeStruct((CX, CY, CZ), f32),
        ),
        in_specs=[anywhere, anywhere, anywhere, vmem, vmem, vmem],
        out_specs=(vmem, vmem),
        scratch_shapes=[
            pltpu.VMEM((7, CX + 2, CY, CZ), f32),
            pltpu.VMEM((3, CX + 2, CY, CZ), f32),
            pltpu.VMEM((3, CX + 2, CY, CZ), f32),
            pltpu.VMEM((7, 2, CX, CZ), f32),
            pltpu.VMEM((7, 2, CX, CZ), f32),
            pltpu.VMEM((3, 2, CX, CZ), f32),
            pltpu.VMEM((3, 2, NG, 1, 128), f32),
            pltpu.VMEM((3, NB, 8, 128), f32),
            pltpu.VMEM((128, 1024), bf16),
            pltpu.VMEM((128, 1024), bf16),
            pltpu.SemaphoreType.DMA((3,)),
            pltpu.SemaphoreType.DMA((7, 4)),
            pltpu.SemaphoreType.DMA((7, 4)),
            pltpu.SemaphoreType.DMA((3, NG)),
            pltpu.SemaphoreType.DMA((3, NG)),
            pltpu.SemaphoreType.DMA((3, NB)),
            pltpu.SemaphoreType.DMA((3, NB)),
        ],
        compiler_params=pltpu.CompilerParams(
            collective_id=0, has_side_effects=True, vmem_limit_bytes=48 * 1024 * 1024),
    )(
        state, diffusivity, sensitivity, patches.reshape(64, 128),
        entries.reshape(8, 128), jnp.swapaxes(table[0], 0, 1),
    )
    return flux.reshape(-1), adjoint


def solution(mesh):
    return jax.shard_map(
        shards,
        mesh=mesh,
        in_specs=(
            P("gx", "bulk", None),
            P("gx", "bulk", None),
            P(("gx", "bulk")),
            P("gx", "bulk"),
            P(("gx", "bulk"), None, None),
            P("gx", "bulk", None),
        ),
        out_specs=(P(("gx", "bulk")), P("gx", "bulk", None)),
        check_vma=False,
    )
```

```python
import jax
import jax.numpy as jnp
from jax import lax
from jax.experimental import pallas as pl
from jax.experimental.pallas import tpu as pltpu
from jax.sharding import PartitionSpec as P

MESH = pl.DeviceIdType.MESH
RATE = 0.08
DRIFT = 0.2
SOURCE = 0.5
HALF_RATE = 0.5 * RATE

NG, NB = 8, 16
CX, CY, CZ = 32, 32, 256

T0, DD, L3, T1, T2, L2, L1 = range(7)


def split3(x):
    hi = x.astype(jnp.bfloat16)
    rest = x - hi.astype(jnp.float32)
    mid = rest.astype(jnp.bfloat16)
    low = (rest - mid.astype(jnp.float32)).astype(jnp.bfloat16)
    return hi, mid, low


def iota(shape, axis):
    return lax.broadcasted_iota(jnp.int32, shape, axis)


def kernel(
    t0_hbm, d_hbm, l3_hbm, patch_ref, entry_ref, table_ref,
    flux_ref, adj_ref,
    fld, kay, slp, yrecv, ysend, kyh, kyf, syf, delta, outbox, inbox, hot_e, hot_p,
    load_sem, xs_sem, xr_sem, a_send, a_recv,
):
    g = lax.axis_index("gx")
    b = lax.axis_index("bulk")
    me = g * NB + b

    inputs = ((T0, t0_hbm), (DD, d_hbm), (L3, l3_hbm))
    edge_loads = [
        [pltpu.make_async_copy(src.at[:, y, :], ysend.at[f, side], load_sem.at[f, side])
         for side, y in ((0, 0), (1, CY - 1))]
        for f, src in inputs
    ]
    loads = [
        pltpu.make_async_copy(src, fld.at[f, pl.ds(1, CX)], load_sem.at[f, 2])
        for f, src in inputs
    ]
    for pair in edge_loads:
        for load in pair:
            load.start()
    for load in loads:
        load.start()
    barrier = pltpu.get_barrier_semaphore()

    def each_other(act):
        for j in range(1, NB):
            act(g, lax.rem(b + j, NB))

        def body(i, _):
            for j in range(NB):
                act(lax.rem(g + i, NG), lax.rem(b + j, NB))
            return 0
        lax.fori_loop(1, NG, body, 0)

    each_other(lambda tg, tb: pl.semaphore_signal(
        barrier, inc=1, device_id=(tg, tb), device_id_type=MESH))

    def post(n, block):
        outbox[n] = jnp.concatenate([block, jnp.zeros((120, 128), jnp.float32)], axis=0).T

        def act(tg, tb):
            pltpu.make_async_remote_copy(
                src_ref=outbox.at[n, pl.ds(tg * NB + tb, 1)], dst_ref=inbox.at[n, pl.ds(me, 1)],
                send_sem=a_send.at[n], recv_sem=a_recv.at[n],
                device_id=(tg, tb), device_id_type=MESH).start()
        each_other(act)
        inbox[n, pl.ds(me, 1)] = outbox[n, pl.ds(me, 1)]

    def everything(n):
        return pltpu.make_async_remote_copy(
            src_ref=outbox.at[n, pl.ds(0, NG * NB - 1)], dst_ref=inbox.at[n, pl.ds(0, NG * NB - 1)],
            send_sem=a_send.at[n], recv_sem=a_recv.at[n],
            device_id=(g, b), device_id_type=MESH)

    def collect(n):
        everything(n).wait_recv()
        return inbox[n].T[0:8]

    def make_hot(hot, low):
        for q in range(8):
            hit = iota((128, 128), 0) == low[q:q + 1, :]
            hot[:, q * 128:(q + 1) * 128] = jnp.where(hit, 1.0, 0.0).astype(jnp.bfloat16)

    def lookup(parts, hot, high, count):
        stacked = jnp.concatenate(parts, axis=0)
        found = jnp.dot(stacked, hot[...], preferred_element_type=jnp.float32)
        total = found[:count] + found[count:2 * count] + found[2 * count:]
        out = []
        for q in range(8):
            piece = total[:, q * 128:(q + 1) * 128]
            hit = iota((count, 128), 0) == high[q:q + 1, :]
            out.append(jnp.sum(jnp.where(hit, piece, 0.0), axis=0, keepdims=True))
        return jnp.concatenate(out, axis=0)

    def scatter(values, hot, high, count):
        spread = jnp.concatenate(
            [jnp.where(iota((count, 128), 0) == high[q:q + 1, :], values[q:q + 1, :], 0.0)
             for q in range(8)], axis=1)
        total = jnp.zeros((count, 128), jnp.float32)
        for part in split3(spread):
            total = total + lax.dot_general(
                part, hot[...], (((1,), (1,)), ((), ())), preferred_element_type=jnp.float32)
        return total

    def zero_edges():
        for edge, plane, side in ((g == 0, 0, None), (g == NG - 1, CX + 1, None),
                                  (b == 0, None, 0), (b == NB - 1, None, 1)):
            @pl.when(edge)
            def _():
                for f in range(7):
                    if plane is not None:
                        fld[f, plane] = jnp.zeros((CY, CZ), jnp.float32)
                    else:
                        yrecv[f, side] = jnp.zeros((CX, CZ), jnp.float32)

    def faces(f):
        def remote(src, dst, way, target):
            return pltpu.make_async_remote_copy(
                src_ref=src, dst_ref=dst, send_sem=xs_sem.at[f, way], recv_sem=xr_sem.at[f, way],
                device_id=target, device_id_type=MESH)
        return (
            (g > 0, g < NG - 1, remote(fld.at[f, 1], fld.at[f, CX + 1], 0, (lax.max(g - 1, 0), b))),
            (g < NG - 1, g > 0, remote(fld.at[f, CX], fld.at[f, 0], 1, (lax.min(g + 1, NG - 1), b))),
            (b > 0, b < NB - 1, remote(ysend.at[f, 0], yrecv.at[f, 1], 2, (g, lax.max(b - 1, 0)))),
            (b < NB - 1, b > 0, remote(ysend.at[f, 1], yrecv.at[f, 0], 3, (g, lax.min(b + 1, NB - 1)))),
        )

    def send(f):
        for sends, _, c in faces(f):
            @pl.when(sends)
            def _():
                c.start()

    def arrive(f):
        for _, receives, c in faces(f):
            @pl.when(receives)
            def _():
                c.wait_recv()

    def sent(f):
        for sends, _, c in faces(f):
            @pl.when(sends)
            def _():
                c.wait_send()

    row = iota((CY, CZ), 0)
    col = iota((CY, CZ), 1)

    def y_down(a):
        return pltpu.roll(a, 1, axis=0)

    def y_up(a):
        return pltpu.roll(a, CY - 1, axis=0)

    def k_down(a):
        return pltpu.roll(a, 1, axis=1)

    def k_up(a):
        return pltpu.roll(a, CZ - 1, axis=1)

    def planes(step, carry):
        carry = lax.fori_loop(1, CX - 3, lambda x, c: step(x, c, False), carry, unroll=4)
        for x in range(CX - 3, CX + 1):
            carry = step(x, carry, x == CX)

    def conduct(n, f):
        def body(x, _):
            h = jnp.tanh(fld[f, x])
            d = fld[DD, x] * HALF_RATE
            kay[n, x] = d + (0.5 * d) * h
            slp[n, x] = (0.5 * d) * (1.0 - h * h)
            return 0
        lax.fori_loop(1, CX + 1, body, 0, unroll=4)

    def conduct_own(n, f):
        for side in range(2):
            h = jnp.tanh(ysend[f, side])
            d = ysend[DD, side] * HALF_RATE
            kyf[n, side] = d + (0.5 * d) * h
            syf[n, side] = (0.5 * d) * (1.0 - h * h)

    def conduct_halo(n, f):
        for x in (0, CX + 1):
            kay[n, x] = HALF_RATE * fld[DD, x] * (1.0 + 0.5 * jnp.tanh(fld[f, x]))
        for side in range(2):
            kyh[n, side] = HALF_RATE * yrecv[DD, side] * (1.0 + 0.5 * jnp.tanh(yrecv[f, side]))

    def forward(n, f, out):
        def step(x, flow_low, last):
            t, k = fld[f, x], kay[n, x]
            acc = (1.0 - DRIFT) * t - flow_low[0] + flow_low[1]
            flow = None
            if not last:
                flow = (k + kay[n, x + 1]) * (fld[f, x + 1] - t)
                acc = acc + flow
            y_l = jnp.where(row == 0, 0.0, (k + y_down(k)) * (t - y_down(t)))
            acc = acc + (y_up(y_l) - y_l)
            kt = k * t
            k_l = jnp.where(col == 0, kt, (k + k_down(k)) * (t - k_down(t)))
            acc = acc + (jnp.where(col == CZ - 1, -kt, k_up(k_l)) - k_l)
            fld[out, x] = acc
            return flow, DRIFT * t
        zero = jnp.zeros((CY, CZ), jnp.float32)
        planes(step, (zero, zero))

    def forward_faces(n, f, out):
        low, high = fld[f, 0], fld[f, CX + 1]
        fld[out, 1] = fld[out, 1] + DRIFT * low - (kay[n, 0] + kay[n, 1]) * (fld[f, 1] - low)
        fld[out, CX] = fld[out, CX] + (kay[n, CX] + kay[n, CX + 1]) * (high - fld[f, CX])
        for side in range(2):
            delta[side] = (kyf[n, side] + kyh[n, side]) * (yrecv[f, side] - ysend[f, side])

    def reverse(n, f, lam, out):
        def step(x, carry, last):
            g_x, m_x = carry
            t, k, l = fld[f, x], kay[n, x], fld[lam, x]
            bend = g_x
            acc = (1.0 - DRIFT) * l + m_x
            g_u = m_u = None
            if not last:
                l_up = fld[lam, x + 1]
                w = l - l_up
                g_u = w * (fld[f, x + 1] - t)
                m_u = w * (k + kay[n, x + 1])
                bend = bend + g_u
                acc = acc + (DRIFT * l_up - m_u)
            w = jnp.where(row == 0, 0.0, y_down(l) - l)
            g_l = w * (t - y_down(t))
            m_l = w * (k + y_down(k))
            bend = bend + (g_l + y_up(g_l))
            acc = acc + (m_l - y_up(m_l))
            lt, lk = l * t, l * k
            w = k_down(l) - l
            g_l = jnp.where(col == 0, -lt, w * (t - k_down(t)))
            m_l = jnp.where(col == 0, -lk, w * (k + k_down(k)))
            bend = bend + (g_l + jnp.where(col == CZ - 1, -lt, k_up(g_l)))
            acc = acc + (m_l - jnp.where(col == CZ - 1, lk, k_up(m_l)))
            value = acc + slp[n, x] * bend
            if out is None:
                adj_ref[x - 1] = value
            else:
                fld[out, x] = value
            return g_u, m_u
        zero = jnp.zeros((CY, CZ), jnp.float32)
        planes(step, (zero, zero))

    def reverse_faces(n, f, lam, out):
        w = fld[lam, 0] - fld[lam, 1]
        low = (slp[n, 1] * (w * (fld[f, 1] - fld[f, 0])) + w * (kay[n, 0] + kay[n, 1]))
        w = fld[lam, CX] - fld[lam, CX + 1]
        high = (slp[n, CX] * (w * (fld[f, CX + 1] - fld[f, CX])) - w * (kay[n, CX] + kay[n, CX + 1])
                + DRIFT * fld[lam, CX + 1])
        if out is None:
            adj_ref[0] = adj_ref[0] + low
            adj_ref[CX - 1] = adj_ref[CX - 1] + high
        else:
            fld[out, 1] = fld[out, 1] + low
            fld[out, CX] = fld[out, CX] + high
        for side in range(2):
            w = yrecv[lam, side] - ysend[lam, side]
            bend = w * (ysend[f, side] - yrecv[f, side])
            delta[side] = syf[n, side] * bend + w * (kyf[n, side] + kyh[n, side])

    def add_delta(f):
        def body(x, _):
            for side, y in ((0, slice(0, 1)), (1, slice(CY - 1, CY))):
                if f is None:
                    adj_ref[x, y] = adj_ref[x, y] + delta[side, pl.ds(x, 1), :]
                else:
                    new = fld[f, x + 1, y] + delta[side, pl.ds(x, 1), :]
                    fld[f, x + 1, y] = new
                    ysend[f, side, pl.ds(x, 1), :] = new
            return 0
        lax.fori_loop(0, CX, body, 0, unroll=4)

    def add_heat(f, columns):
        top = iota((CY, 128), 1) == 0
        for x in range(CX):
            c = columns[(x % 4) * CY:(x % 4 + 1) * CY, x // 4:x // 4 + 1]
            fld[f, x + 1, :, 0:128] = fld[f, x + 1, :, 0:128] + jnp.where(top, SOURCE * c, 0.0)

    def surface(f):
        wide = iota((128, 128), 1)
        total = jnp.zeros((128, 128), jnp.float32)
        for q in range(8):
            block = jnp.concatenate([fld[f, 4 * q + j + 1, :, 0:128] for j in range(4)], axis=0)
            total = total + jnp.where(wide == q, pltpu.roll(block, q, axis=1) if q else block, 0.0)
        return total.T[0:8, :]

    zero_edges()
    table = table_ref[...].astype(jnp.float32)
    pl.semaphore_wait(barrier, NG * NB - 1)
    post(0, table)
    for i, f in ((0, T0), (1, DD), (2, L3)):
        for load in edge_loads[i]:
            load.wait()
        loads[i].wait()
        send(f)
    conduct(0, T0)
    conduct_own(0, T0)
    patches = split3(patch_ref[...])

    spot = collect(0).astype(jnp.int32)
    p_high = spot >> 7
    make_hot(hot_p, spot & 127)
    post(1, lookup(patches, hot_p, p_high, 64))

    forward(0, T0, T1)
    arrive(T0)
    arrive(DD)
    conduct_halo(0, T0)
    forward_faces(0, T0, T1)
    entry = jnp.concatenate([entry_ref[pl.ds(j, 8, stride=4), :] for j in range(4)], axis=1)
    e_high = entry & 7
    make_hot(hot_e, entry >> 3)
    heat = lookup(split3(collect(1)), hot_e, e_high, 8)
    columns = jnp.transpose(heat)
    add_heat(T1, columns)
    add_delta(T1)
    send(T1)
    conduct(1, T1)
    conduct_own(1, T1)
    forward(1, T1, T2)
    add_heat(T2, columns)
    arrive(T1)
    conduct_halo(1, T1)
    forward_faces(1, T1, T2)
    add_delta(T2)
    send(T2)
    conduct(2, T2)
    conduct_own(2, T2)
    reverse(2, T2, L3, L2)
    arrive(L3)
    arrive(T2)
    conduct_halo(2, T2)
    reverse_faces(2, T2, L3, L2)
    add_delta(L2)
    send(L2)
    reverse(1, T1, L2, L1)
    total = surface(L3) + surface(L2)
    arrive(L2)
    reverse_faces(1, T1, L2, L1)
    add_delta(L1)
    send(L1)
    total = total + surface(L1)
    post(2, scatter(SOURCE * total, hot_e, e_high, 8))
    reverse(0, T0, L1, None)
    arrive(L1)
    reverse_faces(0, T0, L1, None)
    add_delta(None)
    flux_ref[...] = scatter(collect(2), hot_p, p_high, 64)

    for n in range(3):
        everything(n).wait_send()
    for f in range(7):
        sent(f)


def shards(state, diffusivity, patches, entries, table, sensitivity):
    anywhere = pl.BlockSpec(memory_space=pl.ANY)
    vmem = pl.BlockSpec(memory_space=pltpu.VMEM)
    f32, bf16 = jnp.float32, jnp.bfloat16
    flux, adjoint = pl.pallas_call(
        kernel,
        out_shape=(
            jax.ShapeDtypeStruct((64, 128), f32),
            jax.ShapeDtypeStruct((CX, CY, CZ), f32),
        ),
        in_specs=[anywhere, anywhere, anywhere, vmem, vmem, vmem],
        out_specs=(vmem, vmem),
        scratch_shapes=[
            pltpu.VMEM((7, CX + 2, CY, CZ), f32),
            pltpu.VMEM((3, CX + 2, CY, CZ), f32),
            pltpu.VMEM((3, CX + 2, CY, CZ), f32),
            pltpu.VMEM((7, 2, CX, CZ), f32),
            pltpu.VMEM((7, 2, CX, CZ), f32),
            pltpu.VMEM((3, 2, CX, CZ), f32),
            pltpu.VMEM((3, 2, CX, CZ), f32),
            pltpu.VMEM((3, 2, CX, CZ), f32),
            pltpu.VMEM((2, CX, CZ), f32),
            pltpu.VMEM((3, NG * NB, 128), f32),
            pltpu.VMEM((3, NG * NB, 128), f32),
            pltpu.VMEM((128, 1024), bf16),
            pltpu.VMEM((128, 1024), bf16),
            pltpu.SemaphoreType.DMA((3, 3)),
            pltpu.SemaphoreType.DMA((7, 4)),
            pltpu.SemaphoreType.DMA((7, 4)),
            pltpu.SemaphoreType.DMA((3,)),
            pltpu.SemaphoreType.DMA((3,)),
        ],
        compiler_params=pltpu.CompilerParams(
            collective_id=0, has_side_effects=True, vmem_limit_bytes=63 * 1024 * 1024),
    )(
        state, diffusivity, sensitivity, patches.reshape(64, 128),
        entries, jnp.swapaxes(table[0], 0, 1),
    )
    return flux.reshape(-1), adjoint


def solution(mesh):
    return jax.shard_map(
        shards,
        mesh=mesh,
        in_specs=(
            P("gx", "bulk", None),
            P("gx", "bulk", None),
            P(("gx", "bulk")),
            P("gx", "bulk"),
            P(("gx", "bulk"), None, None),
            P("gx", "bulk", None),
        ),
        out_specs=(P(("gx", "bulk")), P("gx", "bulk", None)),
        check_vma=False,
    )
```

```python
import jax
import jax.numpy as jnp
from jax import lax
from jax.experimental import pallas as pl
from jax.experimental.pallas import tpu as pltpu
from jax.sharding import PartitionSpec as P

MESH = pl.DeviceIdType.MESH
RATE = 0.08
DRIFT = 0.2
SOURCE = 0.5
HALF_RATE = 0.5 * RATE

NG, NB = 8, 16
CX, CY, CZ = 32, 32, 256

T0, DD, L3, T1, T2, L2, L1 = range(7)

WY = CY + 16
TR = 6 * WY
TL = 384
KAY0, SLP0, TEM1, LAM1, LAM0 = range(5)


def split3(x):
    hi = x.astype(jnp.bfloat16)
    rest = x - hi.astype(jnp.float32)
    mid = rest.astype(jnp.bfloat16)
    low = (rest - mid.astype(jnp.float32)).astype(jnp.bfloat16)
    return hi, mid, low


def iota(shape, axis):
    return lax.broadcasted_iota(jnp.int32, shape, axis)


def kernel(
    t0_hbm, d_hbm, l3_hbm, patch_ref, entry_ref, table_ref,
    flux_ref, adj_ref,
    fld, kay, slp, yrecv, ysend, kyh, kyf, syf, delta, outbox, inbox, hot_n, hot_p, top, nst, turn,
    load_sem, xs_sem, xr_sem, a_send, a_recv, t_send, t_recv,
):
    g = lax.axis_index("gx")
    b = lax.axis_index("bulk")
    me = g * NB + b

    inputs = ((T0, t0_hbm), (DD, d_hbm), (L3, l3_hbm))
    edge_loads = [
        [pltpu.make_async_copy(src.at[:, y, :], ysend.at[f, side], load_sem.at[f, side])
         for side, y in ((0, 0), (1, CY - 1))]
        for f, src in inputs
    ]
    loads = [
        pltpu.make_async_copy(src, fld.at[f, pl.ds(1, CX)], load_sem.at[f, 2])
        for f, src in inputs
    ]
    for pair in edge_loads:
        for load in pair:
            load.start()
    for load in loads:
        load.start()
    barrier = pltpu.get_barrier_semaphore()

    def each_other(act):
        for j in range(1, NB):
            act(g, lax.rem(b + j, NB))

        def body(i, _):
            for j in range(NB):
                act(lax.rem(g + i, NG), lax.rem(b + j, NB))
            return 0
        lax.fori_loop(1, NG, body, 0)

    each_other(lambda tg, tb: pl.semaphore_signal(
        barrier, inc=1, device_id=(tg, tb), device_id_type=MESH))

    def post(n, block):
        pad = jnp.zeros((128 - block.shape[0], 128), jnp.float32)
        outbox[n] = jnp.concatenate([block, pad], axis=0).T

        def act(tg, tb):
            pltpu.make_async_remote_copy(
                src_ref=outbox.at[n, pl.ds(tg * NB + tb, 1)], dst_ref=inbox.at[n, pl.ds(me, 1)],
                send_sem=a_send.at[n], recv_sem=a_recv.at[n],
                device_id=(tg, tb), device_id_type=MESH).start()
        each_other(act)
        inbox[n, pl.ds(me, 1)] = outbox[n, pl.ds(me, 1)]

    def everything(n):
        return pltpu.make_async_remote_copy(
            src_ref=outbox.at[n, pl.ds(0, NG * NB - 1)], dst_ref=inbox.at[n, pl.ds(0, NG * NB - 1)],
            send_sem=a_send.at[n], recv_sem=a_recv.at[n],
            device_id=(g, b), device_id_type=MESH)

    def collect(n, count):
        everything(n).wait_recv()
        return inbox[n].T[0:count]

    def make_hot(hot, low):
        for q in range(8):
            hit = iota((128, 128), 0) == low[q:q + 1, :]
            hot[:, q * 128:(q + 1) * 128] = jnp.where(hit, 1.0, 0.0).astype(jnp.bfloat16)

    def lookup(parts, hot, high, count):
        stacked = jnp.concatenate(parts, axis=0)
        found = jnp.dot(stacked, hot[...], preferred_element_type=jnp.float32)
        total = found[:count] + found[count:2 * count] + found[2 * count:]
        out = []
        for q in range(8):
            piece = total[:, q * 128:(q + 1) * 128]
            hit = iota((count, 128), 0) == high[q:q + 1, :]
            out.append(jnp.sum(jnp.where(hit, piece, 0.0), axis=0, keepdims=True))
        return jnp.concatenate(out, axis=0)

    def scatter(values, hot, high, count):
        spread = jnp.concatenate(
            [jnp.where(iota((count, 128), 0) == high[q:q + 1, :], values[q:q + 1, :], 0.0)
             for q in range(8)], axis=1)
        total = jnp.zeros((count, 128), jnp.float32)
        for part in split3(spread):
            total = total + lax.dot_general(
                part, hot[...], (((1,), (1,)), ((), ())), preferred_element_type=jnp.float32)
        return total

    def zero_edges():
        for edge, plane, side in ((g == 0, 0, None), (g == NG - 1, CX + 1, None),
                                  (b == 0, None, 0), (b == NB - 1, None, 1)):
            @pl.when(edge)
            def _():
                for f in range(7):
                    if plane is not None:
                        fld[f, plane] = jnp.zeros((CY, CZ), jnp.float32)
                    else:
                        yrecv[f, side] = jnp.zeros((CX, CZ), jnp.float32)

    def faces(f):
        def remote(src, dst, way, target):
            return pltpu.make_async_remote_copy(
                src_ref=src, dst_ref=dst, send_sem=xs_sem.at[f, way], recv_sem=xr_sem.at[f, way],
                device_id=target, device_id_type=MESH)
        return (
            (g > 0, g < NG - 1, remote(fld.at[f, 1], fld.at[f, CX + 1], 0, (lax.max(g - 1, 0), b))),
            (g < NG - 1, g > 0, remote(fld.at[f, CX], fld.at[f, 0], 1, (lax.min(g + 1, NG - 1), b))),
            (b > 0, b < NB - 1, remote(ysend.at[f, 0], yrecv.at[f, 1], 2, (g, lax.max(b - 1, 0)))),
            (b < NB - 1, b > 0, remote(ysend.at[f, 1], yrecv.at[f, 0], 3, (g, lax.min(b + 1, NB - 1)))),
        )

    def send(f):
        for sends, _, c in faces(f):
            @pl.when(sends)
            def _():
                c.start()

    def arrive(f):
        for _, receives, c in faces(f):
            @pl.when(receives)
            def _():
                c.wait_recv()

    def sent(f):
        for sends, _, c in faces(f):
            @pl.when(sends)
            def _():
                c.wait_send()

    row = iota((CY, CZ), 0)
    col = iota((CY, CZ), 1)

    def y_down(a):
        return pltpu.roll(a, 1, axis=0)

    def y_up(a):
        return pltpu.roll(a, CY - 1, axis=0)

    def k_down(a):
        return pltpu.roll(a, 1, axis=1)

    def k_up(a):
        return pltpu.roll(a, CZ - 1, axis=1)

    def planes(step, carry):
        carry = lax.fori_loop(1, CX - 3, lambda x, c: step(x, c, False), carry, unroll=4)
        for x in range(CX - 3, CX + 1):
            carry = step(x, carry, x == CX)

    def conduct(n, f):
        def body(x, _):
            h = jnp.tanh(fld[f, x])
            d = fld[DD, x] * HALF_RATE
            kay[n, x] = d + (0.5 * d) * h
            slp[n, x] = (0.5 * d) * (1.0 - h * h)
            return 0
        lax.fori_loop(1, CX + 1, body, 0, unroll=4)

    def conduct_own(n, f):
        for side in range(2):
            h = jnp.tanh(ysend[f, side])
            d = ysend[DD, side] * HALF_RATE
            kyf[n, side] = d + (0.5 * d) * h
            syf[n, side] = (0.5 * d) * (1.0 - h * h)

    def conduct_halo(n, f):
        for x in (0, CX + 1):
            kay[n, x] = HALF_RATE * fld[DD, x] * (1.0 + 0.5 * jnp.tanh(fld[f, x]))
        for side in range(2):
            kyh[n, side] = HALF_RATE * yrecv[DD, side] * (1.0 + 0.5 * jnp.tanh(yrecv[f, side]))

    def forward(n, f, out):
        def step(x, flow_low, last):
            t, k = fld[f, x], kay[n, x]
            acc = (1.0 - DRIFT) * t - flow_low[0] + flow_low[1]
            flow = None
            if not last:
                flow = (k + kay[n, x + 1]) * (fld[f, x + 1] - t)
                acc = acc + flow
            y_l = jnp.where(row == 0, 0.0, (k + y_down(k)) * (t - y_down(t)))
            acc = acc + (y_up(y_l) - y_l)
            kt = k * t
            k_l = jnp.where(col == 0, kt, (k + k_down(k)) * (t - k_down(t)))
            acc = acc + (jnp.where(col == CZ - 1, -kt, k_up(k_l)) - k_l)
            fld[out, x] = acc
            return flow, DRIFT * t
        zero = jnp.zeros((CY, CZ), jnp.float32)
        planes(step, (zero, zero))

    def forward_faces(n, f, out):
        low, high = fld[f, 0], fld[f, CX + 1]
        fld[out, 1] = fld[out, 1] + DRIFT * low - (kay[n, 0] + kay[n, 1]) * (fld[f, 1] - low)
        fld[out, CX] = fld[out, CX] + (kay[n, CX] + kay[n, CX + 1]) * (high - fld[f, CX])
        for side in range(2):
            delta[side] = (kyf[n, side] + kyh[n, side]) * (yrecv[f, side] - ysend[f, side])

    def reverse(n, f, lam, out):
        def step(x, carry, last):
            g_x, m_x = carry
            t, k, l = fld[f, x], kay[n, x], fld[lam, x]
            bend = g_x
            acc = (1.0 - DRIFT) * l + m_x
            g_u = m_u = None
            if not last:
                l_up = fld[lam, x + 1]
                w = l - l_up
                g_u = w * (fld[f, x + 1] - t)
                m_u = w * (k + kay[n, x + 1])
                bend = bend + g_u
                acc = acc + (DRIFT * l_up - m_u)
            w = jnp.where(row == 0, 0.0, y_down(l) - l)
            g_l = w * (t - y_down(t))
            m_l = w * (k + y_down(k))
            bend = bend + (g_l + y_up(g_l))
            acc = acc + (m_l - y_up(m_l))
            lt, lk = l * t, l * k
            w = k_down(l) - l
            g_l = jnp.where(col == 0, -lt, w * (t - k_down(t)))
            m_l = jnp.where(col == 0, -lk, w * (k + k_down(k)))
            bend = bend + (g_l + jnp.where(col == CZ - 1, -lt, k_up(g_l)))
            acc = acc + (m_l - jnp.where(col == CZ - 1, lk, k_up(m_l)))
            value = acc + slp[n, x] * bend
            if out is None:
                adj_ref[x - 1] = value
            else:
                fld[out, x] = value
            return g_u, m_u
        zero = jnp.zeros((CY, CZ), jnp.float32)
        planes(step, (zero, zero))

    def reverse_faces(n, f, lam, out):
        w = fld[lam, 0] - fld[lam, 1]
        low = (slp[n, 1] * (w * (fld[f, 1] - fld[f, 0])) + w * (kay[n, 0] + kay[n, 1]))
        w = fld[lam, CX] - fld[lam, CX + 1]
        high = (slp[n, CX] * (w * (fld[f, CX + 1] - fld[f, CX])) - w * (kay[n, CX] + kay[n, CX + 1])
                + DRIFT * fld[lam, CX + 1])
        if out is None:
            adj_ref[0] = adj_ref[0] + low
            adj_ref[CX - 1] = adj_ref[CX - 1] + high
        else:
            fld[out, 1] = fld[out, 1] + low
            fld[out, CX] = fld[out, CX] + high
        for side in range(2):
            w = yrecv[lam, side] - ysend[lam, side]
            bend = w * (ysend[f, side] - yrecv[f, side])
            delta[side] = syf[n, side] * bend + w * (kyf[n, side] + kyh[n, side])

    def add_delta(f):
        def body(x, _):
            for side, y in ((0, slice(0, 1)), (1, slice(CY - 1, CY))):
                if f is None:
                    adj_ref[x, y] = adj_ref[x, y] + delta[side, pl.ds(x, 1), :]
                else:
                    new = fld[f, x + 1, y] + delta[side, pl.ds(x, 1), :]
                    fld[f, x + 1, y] = new
                    ysend[f, side, pl.ds(x, 1), :] = new
            return 0
        lax.fori_loop(0, CX, body, 0, unroll=4)

    wide = iota((TR, 128), 1)
    tall = iota((TR, 128), 0)
    strip = (tall * 1366) >> 16
    inside = tall - WY * strip
    outside = (
        ((strip == 0) & (g == 0)) | ((strip == 5) & (g == NG - 1))
        | ((inside < 8) & (b == 0)) | ((inside >= 8 + CY) & (b == NB - 1))
    )
    surface = (wide & 15) == 0

    def in_grid(a):
        return jnp.where(outside, 0.0, a)

    def next_x(a):
        r = pltpu.roll(a, 112, axis=1)
        return jnp.where(wide < 112, r, jnp.concatenate([r[WY:], r[:WY]], axis=0))

    def last_x(a):
        r = pltpu.roll(a, 16, axis=1)
        return jnp.where(wide >= 16, r, jnp.concatenate([r[TR - WY:], r[:TR - WY]], axis=0))

    def next_y(a):
        return pltpu.roll(a, TR - 1, axis=0)

    def last_y(a):
        return pltpu.roll(a, 1, axis=0)

    def next_k(a):
        return pltpu.roll(a, 127, axis=1)

    def last_k(a):
        return pltpu.roll(a, 1, axis=1)

    def top_conduct(t, d):
        h = jnp.tanh(t)
        d = d * HALF_RATE
        return d + (0.5 * d) * h, (0.5 * d) * (1.0 - h * h)

    def top_forward(t, k):
        flow = (k + next_x(k)) * (next_x(t) - t)
        acc = (1.0 - DRIFT) * t + DRIFT * last_x(t) + (flow - last_x(flow))
        flow = (k + next_y(k)) * (next_y(t) - t)
        acc = acc + (flow - last_y(flow))
        flow = jnp.where(surface, k * t, (k + last_k(k)) * (t - last_k(t)))
        return acc + (next_k(flow) - flow)

    def top_reverse(t, k, s, l):
        l_up = next_x(l)
        w = l - l_up
        bent = w * (next_x(t) - t)
        moved = w * (k + next_x(k))
        bend = bent + last_x(bent)
        acc = (1.0 - DRIFT) * l + DRIFT * l_up + (last_x(moved) - moved)
        w = l - next_y(l)
        bent = w * (next_y(t) - t)
        moved = w * (k + next_y(k))
        bend = bend + (bent + last_y(bent))
        acc = acc + (last_y(moved) - moved)
        w = last_k(l) - l
        bent = jnp.where(surface, -(l * t), w * (t - last_k(t)))
        moved = jnp.where(surface, -(l * k), w * (k + last_k(k)))
        bend = bend + (bent + next_k(bent))
        acc = acc + (moved - next_k(moved))
        return in_grid(acc + s * bend)

    def top_pack():
        lane = iota((CY, 128), 1) >> 4
        for i, f in enumerate((T0, DD, L3)):
            for strip_x in range(4):
                x = 1 + 8 * strip_x
                tile = fld[f, x, :, 0:128]
                for j in range(1, 8):
                    tile = jnp.where(lane == j, pltpu.roll(fld[f, x + j, :, 0:128], 16 * j, axis=1), tile)
                top[i, 1 + strip_x, 8:8 + CY] = tile
        entry = jnp.concatenate([entry_ref[...], jnp.zeros((CX, 128 - CY), jnp.int32)], axis=1)
        entry = jnp.concatenate([entry.astype(jnp.float32), jnp.zeros((128 - CX, 128), jnp.float32)], axis=0)
        entry = entry.T[0:CY].astype(jnp.int32)
        spread = jnp.where(iota((128, 512), 0) == (iota((128, 512), 1) >> 4), 1.0, 0.0).astype(jnp.bfloat16)
        high = jnp.dot((entry >> 3).astype(jnp.float32).astype(jnp.bfloat16), spread,
                       preferred_element_type=jnp.float32)
        low = jnp.dot((entry & 7).astype(jnp.float32).astype(jnp.bfloat16), spread,
                      preferred_element_type=jnp.float32)
        entry = 8.0 * high + low
        for strip_x in range(4):
            top[3, 1 + strip_x, 8:8 + CY] = entry[:, 128 * strip_x:128 * (strip_x + 1)]

    def top_copies():
        out = []
        along_x = {-1: (1, 1, 5), 0: (1, 4, 1), 1: (4, 1, 0)}
        along_y = {-1: (8, 8, 8 + CY), 0: (8, CY, 8), 1: (CY, 8, 0)}
        for dx in (-1, 0, 1):
            for dy in (-1, 0, 1):
                if dx == 0 and dy == 0:
                    continue
                way = (dx + 1) * 3 + dy + 1
                x, wide_x, to_x = along_x[dx]
                y, wide_y, to_y = along_y[dy]
                sends, receives = None, None
                for d, at, size in ((dx, g, NG), (dy, b, NB)):
                    if d:
                        one = (at > 0, at < size - 1)
                        one = one if d < 0 else one[::-1]
                        sends = one[0] if sends is None else sends & one[0]
                        receives = one[1] if receives is None else receives & one[1]
                target = (lax.clamp(0, g + dx, NG - 1), lax.clamp(0, b + dy, NB - 1))
                out.append((sends, receives, pltpu.make_async_remote_copy(
                    src_ref=top.at[:, pl.ds(x, wide_x), pl.ds(y, wide_y)],
                    dst_ref=top.at[:, pl.ds(to_x, wide_x), pl.ds(to_y, wide_y)],
                    send_sem=t_send.at[way], recv_sem=t_recv.at[way],
                    device_id=target, device_id_type=MESH)))
        return out

    def when(condition, action):
        @pl.when(condition)
        def _():
            action()

    line = iota((1, TL), 1)
    line_strip = (line * 1366) >> 16
    line_y = line - WY * line_strip
    side_x = jnp.where(line_strip == 0, 0, jnp.where(line_strip >= 5, 2, 1))
    side_y = jnp.where(line_y < 8, 0, jnp.where(line_y >= 8 + CY, 2, 1))
    whose = 3 * side_x + side_y
    ours = whose == 4

    def to_lines(a):
        turned = jnp.concatenate([a, jnp.zeros((TL - TR, 128), jnp.float32)], axis=0).T
        return jnp.concatenate([turned[16 * j:16 * j + 1] for j in range(8)], axis=0)

    def from_lines(lines):
        turn[...] = jnp.zeros((128, TL), jnp.float32)
        for j in range(8):
            turn[16 * j:16 * j + 1, :] = lines[j]
        return turn[...].T[0:TR]

    def neighbours(v):
        return jnp.concatenate(
            [pltpu.roll(v, (-(NB * dx + dy)) % 128, axis=1) if dx or dy else v
             for dx in (-1, 0, 1) for dy in (-1, 0, 1)], axis=0)

    def top_hot(entry):
        for j in range(8):
            hit = iota((128, TL), 0) == (entry[j:j + 1] >> 3)
            hot_n[:, j * TL:(j + 1) * TL] = jnp.where(hit, 1.0, 0.0).astype(jnp.bfloat16)

    def top_heat(slots, entry):
        stacked = jnp.concatenate(split3(slots), axis=0)
        lines = []
        for j in range(8):
            found = jnp.dot(stacked, hot_n[:, j * TL:(j + 1) * TL], preferred_element_type=jnp.float32)
            found = found[:72] + found[72:144] + found[144:]
            hit = iota((72, TL), 0) == 8 * whose + (entry[j:j + 1] & 7)
            lines.append(jnp.sum(jnp.where(hit, found, 0.0), axis=0, keepdims=True))
        return from_lines(lines)

    def top_slots(a, entry):
        lines = to_lines(a)
        spread = jnp.concatenate(
            [jnp.where((iota((8, TL), 0) == (entry[j:j + 1] & 7)) & ours, lines[j:j + 1], 0.0)
             for j in range(8)], axis=1)
        stacked = jnp.concatenate(split3(spread), axis=0)
        total = lax.dot_general(
            stacked, hot_n[...], (((1,), (1,)), ((), ())), preferred_element_type=jnp.float32)
        return total[0:8] + total[8:16] + total[16:24]

    def overlay():
        lane = iota((CY, 128), 1)
        for x in range(CX):
            rows = nst[LAM0, (1 + x // 8) * WY + 8:(1 + x // 8) * WY + 8 + CY]
            j = x % 8
            rows = pltpu.roll(rows, 128 - 16 * j, axis=1) if j else rows
            adj_ref[x, :, 0:128] = jnp.where(lane < 5, rows, adj_ref[x, :, 0:128])

    zero_edges()
    table = table_ref[...].astype(jnp.float32)
    pl.semaphore_wait(barrier, NG * NB - 1)
    post(0, table)
    for i, f in ((0, T0), (1, DD), (2, L3)):
        for load in edge_loads[i]:
            load.wait()
        loads[i].wait()
        send(f)
    top_pack()
    tops = top_copies()
    for sends, _, c in tops:
        when(sends, c.start)
    conduct(0, T0)
    conduct_own(0, T0)
    patches = split3(patch_ref[...])

    spot = collect(0, 8).astype(jnp.int32)
    p_high = spot >> 7
    make_hot(hot_p, spot & 127)
    post(1, neighbours(lookup(patches, hot_p, p_high, 64)))

    forward(0, T0, T1)
    arrive(T0)
    arrive(DD)
    conduct_halo(0, T0)
    forward_faces(0, T0, T1)
    add_delta(T1)
    send(T1)
    conduct(1, T1)
    conduct_own(1, T1)
    forward(1, T1, T2)

    for _, receives, c in tops:
        when(receives, c.wait_recv)
    def whole(i):
        return top[i].reshape(TR, 128)
    t0, d, l3 = in_grid(whole(0)), in_grid(whole(1)), in_grid(whole(2))
    entry = to_lines(whole(3)).astype(jnp.int32)
    top_hot(entry)
    k0, s0 = top_conduct(t0, d)
    nst[KAY0], nst[SLP0] = k0, s0
    nst[TEM1] = top_forward(t0, k0)

    arrive(T1)
    conduct_halo(1, T1)
    forward_faces(1, T1, T2)
    add_delta(T2)
    send(T2)

    heat = SOURCE * top_heat(collect(1, 72), entry)
    t1 = in_grid(nst[TEM1] + heat)
    k1, s1 = top_conduct(t1, d)
    t2 = in_grid(top_forward(t1, k1) + heat)
    k2, s2 = top_conduct(t2, d)
    l2 = top_reverse(t2, k2, s2, l3)
    l1 = top_reverse(t1, k1, s1, l2)
    post(2, top_slots(SOURCE * (l3 + l2 + l1), entry))
    nst[LAM1] = l1

    conduct(2, T2)
    conduct_own(2, T2)
    reverse(2, T2, L3, L2)
    arrive(L3)
    arrive(T2)
    conduct_halo(2, T2)
    reverse_faces(2, T2, L3, L2)
    add_delta(L2)
    send(L2)
    nst[LAM0] = top_reverse(in_grid(whole(0)), nst[KAY0], nst[SLP0], nst[LAM1])
    reverse(1, T1, L2, L1)
    arrive(L2)
    reverse_faces(1, T1, L2, L1)
    add_delta(L1)
    send(L1)
    reverse(0, T0, L1, None)
    flux_ref[...] = scatter(collect(2, 8), hot_p, p_high, 64)
    arrive(L1)
    reverse_faces(0, T0, L1, None)
    add_delta(None)
    overlay()

    for n in range(3):
        everything(n).wait_send()
    for f in range(7):
        sent(f)
    for sends, _, c in tops:
        when(sends, c.wait_send)


def shards(state, diffusivity, patches, entries, table, sensitivity):
    anywhere = pl.BlockSpec(memory_space=pl.ANY)
    vmem = pl.BlockSpec(memory_space=pltpu.VMEM)
    f32, bf16 = jnp.float32, jnp.bfloat16
    flux, adjoint = pl.pallas_call(
        kernel,
        out_shape=(
            jax.ShapeDtypeStruct((64, 128), f32),
            jax.ShapeDtypeStruct((CX, CY, CZ), f32),
        ),
        in_specs=[anywhere, anywhere, anywhere, vmem, vmem, vmem],
        out_specs=(vmem, vmem),
        scratch_shapes=[
            pltpu.VMEM((7, CX + 2, CY, CZ), f32),
            pltpu.VMEM((3, CX + 2, CY, CZ), f32),
            pltpu.VMEM((3, CX + 2, CY, CZ), f32),
            pltpu.VMEM((7, 2, CX, CZ), f32),
            pltpu.VMEM((7, 2, CX, CZ), f32),
            pltpu.VMEM((3, 2, CX, CZ), f32),
            pltpu.VMEM((3, 2, CX, CZ), f32),
            pltpu.VMEM((3, 2, CX, CZ), f32),
            pltpu.VMEM((2, CX, CZ), f32),
            pltpu.VMEM((3, NG * NB, 128), f32),
            pltpu.VMEM((3, NG * NB, 128), f32),
            pltpu.VMEM((128, 8 * TL), bf16),
            pltpu.VMEM((128, 1024), bf16),
            pltpu.VMEM((4, 6, WY, 128), f32),
            pltpu.VMEM((5, TR, 128), f32),
            pltpu.VMEM((128, TL), f32),
            pltpu.SemaphoreType.DMA((3, 3)),
            pltpu.SemaphoreType.DMA((7, 4)),
            pltpu.SemaphoreType.DMA((7, 4)),
            pltpu.SemaphoreType.DMA((3,)),
            pltpu.SemaphoreType.DMA((3,)),
            pltpu.SemaphoreType.DMA((9,)),
            pltpu.SemaphoreType.DMA((9,)),
        ],
        compiler_params=pltpu.CompilerParams(
            collective_id=0, has_side_effects=True, vmem_limit_bytes=63 * 1024 * 1024),
    )(
        state, diffusivity, sensitivity, patches.reshape(64, 128),
        entries, jnp.swapaxes(table[0], 0, 1),
    )
    return flux.reshape(-1), adjoint


def solution(mesh):
    return jax.shard_map(
        shards,
        mesh=mesh,
        in_specs=(
            P("gx", "bulk", None),
            P("gx", "bulk", None),
            P(("gx", "bulk")),
            P("gx", "bulk"),
            P(("gx", "bulk"), None, None),
            P("gx", "bulk", None),
        ),
        out_specs=(P(("gx", "bulk")), P("gx", "bulk", None)),
        check_vma=False,
    )
```

```python
import jax
import jax.numpy as jnp
from jax import lax
from jax.experimental import pallas as pl
from jax.experimental.pallas import tpu as pltpu
from jax.sharding import PartitionSpec as P

MESH = pl.DeviceIdType.MESH
RATE = 0.08
DRIFT = 0.2
SOURCE = 0.5
HALF_RATE = 0.5 * RATE

NG, NB = 8, 16
CX, CY, CZ = 32, 32, 256

T0, DD, L3, T1, T2, L2, L1 = range(7)

WY = CY + 16
TR = 6 * WY
TL = 384
KAY0, SLP0, TEM1, LAM1, LAM0 = range(5)


def split3(x):
    hi = x.astype(jnp.bfloat16)
    rest = x - hi.astype(jnp.float32)
    mid = rest.astype(jnp.bfloat16)
    low = (rest - mid.astype(jnp.float32)).astype(jnp.bfloat16)
    return hi, mid, low


def iota(shape, axis):
    return lax.broadcasted_iota(jnp.int32, shape, axis)


def kernel(
    t0_hbm, d_hbm, l3_hbm, patch_ref, entry_ref, table_ref,
    flux_ref, adj_ref,
    fld, kay, slp, yrecv, ysend, kyh, kyf, syf, delta, outbox, inbox, rows, gath, hot_n, hot_p, top, nst, turn,
    load_sem, xs_sem, xr_sem, a_send, a_recv, g_send, g_recv, b_send, b_recv, t_send, t_recv,
):
    g = lax.axis_index("gx")
    b = lax.axis_index("bulk")
    me = g * NB + b

    inputs = ((T0, t0_hbm), (DD, d_hbm), (L3, l3_hbm))
    edge_loads = [
        [pltpu.make_async_copy(src.at[:, y, :], ysend.at[f, side], load_sem.at[f, side])
         for side, y in ((0, 0), (1, CY - 1))]
        for f, src in inputs
    ]
    loads = [
        pltpu.make_async_copy(src, fld.at[f, pl.ds(1, CX)], load_sem.at[f, 2])
        for f, src in inputs
    ]
    for pair in edge_loads:
        for load in pair:
            load.start()
    for load in loads:
        load.start()
    barrier = pltpu.get_barrier_semaphore()

    def each_other(act):
        for j in range(1, NB):
            act(g, ((b + j) & (NB - 1)))

        def body(i, _):
            for j in range(NB):
                act(((g + i) & (NG - 1)), ((b + j) & (NB - 1)))
            return 0
        lax.fori_loop(1, NG, body, 0)

    for k in range(1, NG):
        pl.semaphore_signal(barrier, inc=1, device_id=(((g + k) & (NG - 1)), b), device_id_type=MESH)
    for k in range(1, NB):
        pl.semaphore_signal(barrier, inc=1, device_id=(g, ((b + k) & (NB - 1))), device_id_type=MESH)
    corners = [(i, j) for i in (1, NG - 1) for j in (1, NB - 1)]
    for i, j in corners:
        pl.semaphore_signal(
            barrier, inc=1, device_id=(((g + i) & (NG - 1)), ((b + j) & (NB - 1))), device_id_type=MESH)

    def swap(a):
        lane, sub = iota((8, 128), 1), iota((8, 128), 0)
        out = jnp.zeros((8, 128), jnp.float32)
        for k in range(8):
            turned = pltpu.roll(a, 16 * k, axis=1) if k else a
            kept = jnp.where((lane >> 4) == sub, turned, 0.0)
            out = out + (pltpu.roll(kept, 8 - k, axis=0) if k else kept)
        return out

    def stage_one(block):
        rows[0] = block
        rows[1, pl.ds(g, 1)] = rows[0, pl.ds(g, 1)]
        copies = []
        for k in range(1, NG):
            o = ((g + k) & (NG - 1))
            c = pltpu.make_async_remote_copy(
                src_ref=rows.at[0, pl.ds(o, 1)], dst_ref=rows.at[1, pl.ds(g, 1)],
                send_sem=g_send.at[k], recv_sem=g_recv.at[k],
                device_id=(o, b), device_id_type=MESH)
            c.start()
            copies.append(c)
        return copies

    def stage_two(first):
        for c in first:
            c.wait_recv()
        copies = []
        for k in range(1, NB):
            c = pltpu.make_async_remote_copy(
                src_ref=rows.at[1], dst_ref=gath.at[b],
                send_sem=b_send.at[k], recv_sem=b_recv.at[k],
                device_id=(g, ((b + k) & (NB - 1))), device_id_type=MESH)
            c.start()
            copies.append(c)
        gath[b] = rows[1]
        return copies

    def finish(second):
        for c in second:
            c.wait_recv()
        lane = iota((8, 128), 1)
        out = jnp.zeros((8, 128), jnp.float32)
        for k in range(NB):
            turned = pltpu.roll(gath[k], lax.rem(k - b + 128, 128), axis=1)
            out = out + jnp.where((lane & 15) == k, turned, 0.0)
        return swap(out)

    def post(n, block):
        pad = jnp.zeros((128 - block.shape[0], 128), jnp.float32)
        outbox[n] = jnp.concatenate([block, pad], axis=0).T

        def act(tg, tb):
            pltpu.make_async_remote_copy(
                src_ref=outbox.at[n, pl.ds(tg * NB + tb, 1)], dst_ref=inbox.at[n, pl.ds(me, 1)],
                send_sem=a_send.at[n], recv_sem=a_recv.at[n],
                device_id=(tg, tb), device_id_type=MESH).start()
        each_other(act)
        inbox[n, pl.ds(me, 1)] = outbox[n, pl.ds(me, 1)]

    def everything(n):
        return pltpu.make_async_remote_copy(
            src_ref=outbox.at[n, pl.ds(0, NG * NB - 1)], dst_ref=inbox.at[n, pl.ds(0, NG * NB - 1)],
            send_sem=a_send.at[n], recv_sem=a_recv.at[n],
            device_id=(g, b), device_id_type=MESH)

    def collect(n, count):
        everything(n).wait_recv()
        return inbox[n].T[0:count]

    def make_hot(hot, low):
        for q in range(8):
            hit = iota((128, 128), 0) == low[q:q + 1, :]
            hot[:, q * 128:(q + 1) * 128] = jnp.where(hit, 1.0, 0.0).astype(jnp.bfloat16)

    def lookup(parts, hot, high, count):
        stacked = jnp.concatenate(parts, axis=0)
        found = jnp.dot(stacked, hot[...], preferred_element_type=jnp.float32)
        total = found[:count] + found[count:2 * count] + found[2 * count:]
        out = []
        for q in range(8):
            piece = total[:, q * 128:(q + 1) * 128]
            hit = iota((count, 128), 0) == high[q:q + 1, :]
            out.append(jnp.sum(jnp.where(hit, piece, 0.0), axis=0, keepdims=True))
        return jnp.concatenate(out, axis=0)

    def scatter(values, hot, high, count):
        spread = jnp.concatenate(
            [jnp.where(iota((count, 128), 0) == high[q:q + 1, :], values[q:q + 1, :], 0.0)
             for q in range(8)], axis=1)
        total = jnp.zeros((count, 128), jnp.float32)
        for part in split3(spread):
            total = total + lax.dot_general(
                part, hot[...], (((1,), (1,)), ((), ())), preferred_element_type=jnp.float32)
        return total

    def zero_edges():
        for edge, plane, side in ((g == 0, 0, None), (g == NG - 1, CX + 1, None),
                                  (b == 0, None, 0), (b == NB - 1, None, 1)):
            @pl.when(edge)
            def _():
                for f in range(7):
                    if plane is not None:
                        fld[f, plane] = jnp.zeros((CY, CZ), jnp.float32)
                    else:
                        yrecv[f, side] = jnp.zeros((CX, CZ), jnp.float32)

    def faces(f):
        def remote(src, dst, way, target):
            return pltpu.make_async_remote_copy(
                src_ref=src, dst_ref=dst, send_sem=xs_sem.at[f, way], recv_sem=xr_sem.at[f, way],
                device_id=target, device_id_type=MESH)
        return (
            (g > 0, g < NG - 1, remote(fld.at[f, 1], fld.at[f, CX + 1], 0, (lax.max(g - 1, 0), b))),
            (g < NG - 1, g > 0, remote(fld.at[f, CX], fld.at[f, 0], 1, (lax.min(g + 1, NG - 1), b))),
            (b > 0, b < NB - 1, remote(ysend.at[f, 0], yrecv.at[f, 1], 2, (g, lax.max(b - 1, 0)))),
            (b < NB - 1, b > 0, remote(ysend.at[f, 1], yrecv.at[f, 0], 3, (g, lax.min(b + 1, NB - 1)))),
        )

    def send(f):
        for sends, _, c in faces(f):
            @pl.when(sends)
            def _():
                c.start()

    def arrive(f):
        for _, receives, c in faces(f):
            @pl.when(receives)
            def _():
                c.wait_recv()

    def sent(f):
        for sends, _, c in faces(f):
            @pl.when(sends)
            def _():
                c.wait_send()

    row = iota((CY, CZ), 0)
    col = iota((CY, CZ), 1)

    def y_down(a):
        return pltpu.roll(a, 1, axis=0)

    def y_up(a):
        return pltpu.roll(a, CY - 1, axis=0)

    def k_down(a):
        return pltpu.roll(a, 1, axis=1)

    def k_up(a):
        return pltpu.roll(a, CZ - 1, axis=1)

    def planes(step, carry):
        carry = lax.fori_loop(1, CX - 3, lambda x, c: step(x, c, False), carry, unroll=4)
        for x in range(CX - 3, CX + 1):
            carry = step(x, carry, x == CX)

    def conduct(n, f):
        def body(x, _):
            h = jnp.tanh(fld[f, x])
            d = fld[DD, x] * HALF_RATE
            kay[n, x] = d + (0.5 * d) * h
            slp[n, x] = (0.5 * d) * (1.0 - h * h)
            return 0
        lax.fori_loop(1, CX + 1, body, 0, unroll=4)

    def conduct_own(n, f):
        for side in range(2):
            h = jnp.tanh(ysend[f, side])
            d = ysend[DD, side] * HALF_RATE
            kyf[n, side] = d + (0.5 * d) * h
            syf[n, side] = (0.5 * d) * (1.0 - h * h)

    def conduct_halo(n, f):
        for x in (0, CX + 1):
            kay[n, x] = HALF_RATE * fld[DD, x] * (1.0 + 0.5 * jnp.tanh(fld[f, x]))
        for side in range(2):
            kyh[n, side] = HALF_RATE * yrecv[DD, side] * (1.0 + 0.5 * jnp.tanh(yrecv[f, side]))

    def forward(n, f, out):
        def step(x, flow_low, last):
            t, k = fld[f, x], kay[n, x]
            acc = (1.0 - DRIFT) * t - flow_low[0] + flow_low[1]
            flow = None
            if not last:
                flow = (k + kay[n, x + 1]) * (fld[f, x + 1] - t)
                acc = acc + flow
            y_l = jnp.where(row == 0, 0.0, (k + y_down(k)) * (t - y_down(t)))
            acc = acc + (y_up(y_l) - y_l)
            kt = k * t
            k_l = jnp.where(col == 0, kt, (k + k_down(k)) * (t - k_down(t)))
            acc = acc + (jnp.where(col == CZ - 1, -kt, k_up(k_l)) - k_l)
            fld[out, x] = acc
            return flow, DRIFT * t
        zero = jnp.zeros((CY, CZ), jnp.float32)
        planes(step, (zero, zero))

    def forward_faces(n, f, out):
        low, high = fld[f, 0], fld[f, CX + 1]
        fld[out, 1] = fld[out, 1] + DRIFT * low - (kay[n, 0] + kay[n, 1]) * (fld[f, 1] - low)
        fld[out, CX] = fld[out, CX] + (kay[n, CX] + kay[n, CX + 1]) * (high - fld[f, CX])
        for side in range(2):
            delta[side] = (kyf[n, side] + kyh[n, side]) * (yrecv[f, side] - ysend[f, side])

    def reverse(n, f, lam, out):
        def step(x, carry, last):
            g_x, m_x = carry
            t, k, l = fld[f, x], kay[n, x], fld[lam, x]
            bend = g_x
            acc = (1.0 - DRIFT) * l + m_x
            g_u = m_u = None
            if not last:
                l_up = fld[lam, x + 1]
                w = l - l_up
                g_u = w * (fld[f, x + 1] - t)
                m_u = w * (k + kay[n, x + 1])
                bend = bend + g_u
                acc = acc + (DRIFT * l_up - m_u)
            w = jnp.where(row == 0, 0.0, y_down(l) - l)
            g_l = w * (t - y_down(t))
            m_l = w * (k + y_down(k))
            bend = bend + (g_l + y_up(g_l))
            acc = acc + (m_l - y_up(m_l))
            lt, lk = l * t, l * k
            w = k_down(l) - l
            g_l = jnp.where(col == 0, -lt, w * (t - k_down(t)))
            m_l = jnp.where(col == 0, -lk, w * (k + k_down(k)))
            bend = bend + (g_l + jnp.where(col == CZ - 1, -lt, k_up(g_l)))
            acc = acc + (m_l - jnp.where(col == CZ - 1, lk, k_up(m_l)))
            value = acc + slp[n, x] * bend
            if out is None:
                adj_ref[x - 1] = value
            else:
                fld[out, x] = value
            return g_u, m_u
        zero = jnp.zeros((CY, CZ), jnp.float32)
        planes(step, (zero, zero))

    def reverse_faces(n, f, lam, out):
        w = fld[lam, 0] - fld[lam, 1]
        low = (slp[n, 1] * (w * (fld[f, 1] - fld[f, 0])) + w * (kay[n, 0] + kay[n, 1]))
        w = fld[lam, CX] - fld[lam, CX + 1]
        high = (slp[n, CX] * (w * (fld[f, CX + 1] - fld[f, CX])) - w * (kay[n, CX] + kay[n, CX + 1])
                + DRIFT * fld[lam, CX + 1])
        if out is None:
            adj_ref[0] = adj_ref[0] + low
            adj_ref[CX - 1] = adj_ref[CX - 1] + high
        else:
            fld[out, 1] = fld[out, 1] + low
            fld[out, CX] = fld[out, CX] + high
        for side in range(2):
            w = yrecv[lam, side] - ysend[lam, side]
            bend = w * (ysend[f, side] - yrecv[f, side])
            delta[side] = syf[n, side] * bend + w * (kyf[n, side] + kyh[n, side])

    def add_delta(f):
        def body(x, _):
            for side, y in ((0, slice(0, 1)), (1, slice(CY - 1, CY))):
                if f is None:
                    adj_ref[x, y] = adj_ref[x, y] + delta[side, pl.ds(x, 1), :]
                else:
                    new = fld[f, x + 1, y] + delta[side, pl.ds(x, 1), :]
                    fld[f, x + 1, y] = new
                    ysend[f, side, pl.ds(x, 1), :] = new
            return 0
        lax.fori_loop(0, CX, body, 0, unroll=4)

    wide = iota((TR, 128), 1)
    tall = iota((TR, 128), 0)
    strip = (tall * 1366) >> 16
    inside = tall - WY * strip
    outside = (
        ((strip == 0) & (g == 0)) | ((strip == 5) & (g == NG - 1))
        | ((inside < 8) & (b == 0)) | ((inside >= 8 + CY) & (b == NB - 1))
    )
    surface = (wide & 15) == 0

    def in_grid(a):
        return jnp.where(outside, 0.0, a)

    def next_x(a):
        r = pltpu.roll(a, 112, axis=1)
        return jnp.where(wide < 112, r, jnp.concatenate([r[WY:], r[:WY]], axis=0))

    def last_x(a):
        r = pltpu.roll(a, 16, axis=1)
        return jnp.where(wide >= 16, r, jnp.concatenate([r[TR - WY:], r[:TR - WY]], axis=0))

    def next_y(a):
        return pltpu.roll(a, TR - 1, axis=0)

    def last_y(a):
        return pltpu.roll(a, 1, axis=0)

    def next_k(a):
        return pltpu.roll(a, 127, axis=1)

    def last_k(a):
        return pltpu.roll(a, 1, axis=1)

    def top_conduct(t, d):
        h = jnp.tanh(t)
        d = d * HALF_RATE
        return d + (0.5 * d) * h, (0.5 * d) * (1.0 - h * h)

    def top_forward(t, k):
        flow = (k + next_x(k)) * (next_x(t) - t)
        acc = (1.0 - DRIFT) * t + DRIFT * last_x(t) + (flow - last_x(flow))
        flow = (k + next_y(k)) * (next_y(t) - t)
        acc = acc + (flow - last_y(flow))
        flow = jnp.where(surface, k * t, (k + last_k(k)) * (t - last_k(t)))
        return acc + (next_k(flow) - flow)

    def top_reverse(t, k, s, l):
        l_up = next_x(l)
        w = l - l_up
        bent = w * (next_x(t) - t)
        moved = w * (k + next_x(k))
        bend = bent + last_x(bent)
        acc = (1.0 - DRIFT) * l + DRIFT * l_up + (last_x(moved) - moved)
        w = l - next_y(l)
        bent = w * (next_y(t) - t)
        moved = w * (k + next_y(k))
        bend = bend + (bent + last_y(bent))
        acc = acc + (last_y(moved) - moved)
        w = last_k(l) - l
        bent = jnp.where(surface, -(l * t), w * (t - last_k(t)))
        moved = jnp.where(surface, -(l * k), w * (k + last_k(k)))
        bend = bend + (bent + next_k(bent))
        acc = acc + (moved - next_k(moved))
        return in_grid(acc + s * bend)

    def top_pack():
        lane = iota((CY, 128), 1) >> 4
        for i, f in enumerate((T0, DD, L3)):
            for strip_x in range(4):
                x = 1 + 8 * strip_x
                tile = fld[f, x, :, 0:128]
                for j in range(1, 8):
                    tile = jnp.where(lane == j, pltpu.roll(fld[f, x + j, :, 0:128], 16 * j, axis=1), tile)
                top[i, 1 + strip_x, 8:8 + CY] = tile
        entry = jnp.concatenate([entry_ref[...], jnp.zeros((CX, 128 - CY), jnp.int32)], axis=1)
        entry = jnp.concatenate([entry.astype(jnp.float32), jnp.zeros((128 - CX, 128), jnp.float32)], axis=0)
        entry = entry.T[0:CY].astype(jnp.int32)
        spread = jnp.where(iota((128, 512), 0) == (iota((128, 512), 1) >> 4), 1.0, 0.0).astype(jnp.bfloat16)
        high = jnp.dot((entry >> 3).astype(jnp.float32).astype(jnp.bfloat16), spread,
                       preferred_element_type=jnp.float32)
        low = jnp.dot((entry & 7).astype(jnp.float32).astype(jnp.bfloat16), spread,
                      preferred_element_type=jnp.float32)
        entry = 8.0 * high + low
        for strip_x in range(4):
            top[3, 1 + strip_x, 8:8 + CY] = entry[:, 128 * strip_x:128 * (strip_x + 1)]

    def top_copies():
        out = []
        along_x = {-1: (1, 1, 5), 0: (1, 4, 1), 1: (4, 1, 0)}
        along_y = {-1: (8, 8, 8 + CY), 0: (8, CY, 8), 1: (CY, 8, 0)}
        for dx in (-1, 0, 1):
            for dy in (-1, 0, 1):
                if dx == 0 and dy == 0:
                    continue
                way = (dx + 1) * 3 + dy + 1
                x, wide_x, to_x = along_x[dx]
                y, wide_y, to_y = along_y[dy]
                sends, receives = None, None
                for d, at, size in ((dx, g, NG), (dy, b, NB)):
                    if d:
                        one = (at > 0, at < size - 1)
                        one = one if d < 0 else one[::-1]
                        sends = one[0] if sends is None else sends & one[0]
                        receives = one[1] if receives is None else receives & one[1]
                target = (lax.clamp(0, g + dx, NG - 1), lax.clamp(0, b + dy, NB - 1))
                out.append((sends, receives, pltpu.make_async_remote_copy(
                    src_ref=top.at[:, pl.ds(x, wide_x), pl.ds(y, wide_y)],
                    dst_ref=top.at[:, pl.ds(to_x, wide_x), pl.ds(to_y, wide_y)],
                    send_sem=t_send.at[way], recv_sem=t_recv.at[way],
                    device_id=target, device_id_type=MESH)))
        return out

    def when(condition, action):
        @pl.when(condition)
        def _():
            action()

    line = iota((1, TL), 1)
    line_strip = (line * 1366) >> 16
    line_y = line - WY * line_strip
    side_x = jnp.where(line_strip == 0, 0, jnp.where(line_strip >= 5, 2, 1))
    side_y = jnp.where(line_y < 8, 0, jnp.where(line_y >= 8 + CY, 2, 1))
    whose = 3 * side_x + side_y
    ours = whose == 4

    def to_lines(a):
        turned = jnp.concatenate([a, jnp.zeros((TL - TR, 128), jnp.float32)], axis=0).T
        return jnp.concatenate([turned[16 * j:16 * j + 1] for j in range(8)], axis=0)

    def from_lines(lines):
        turn[...] = jnp.zeros((128, TL), jnp.float32)
        for j in range(8):
            turn[16 * j:16 * j + 1, :] = lines[j]
        return turn[...].T[0:TR]

    def neighbours(v):
        return jnp.concatenate(
            [pltpu.roll(v, (-(NB * dx + dy)) % 128, axis=1) if dx or dy else v
             for dx in (-1, 0, 1) for dy in (-1, 0, 1)], axis=0)

    def top_hot(entry):
        for j in range(8):
            hit = iota((128, TL), 0) == (entry[j:j + 1] >> 3)
            hot_n[:, j * TL:(j + 1) * TL] = jnp.where(hit, 1.0, 0.0).astype(jnp.bfloat16)

    def top_heat(slots, entry):
        stacked = jnp.concatenate(split3(slots), axis=0)
        lines = []
        for j in range(8):
            found = jnp.dot(stacked, hot_n[:, j * TL:(j + 1) * TL], preferred_element_type=jnp.float32)
            found = found[:72] + found[72:144] + found[144:]
            hit = iota((72, TL), 0) == 8 * whose + (entry[j:j + 1] & 7)
            lines.append(jnp.sum(jnp.where(hit, found, 0.0), axis=0, keepdims=True))
        return from_lines(lines)

    def top_slots(a, entry):
        lines = to_lines(a)
        spread = jnp.concatenate(
            [jnp.where((iota((8, TL), 0) == (entry[j:j + 1] & 7)) & ours, lines[j:j + 1], 0.0)
             for j in range(8)], axis=1)
        stacked = jnp.concatenate(split3(spread), axis=0)
        total = lax.dot_general(
            stacked, hot_n[...], (((1,), (1,)), ((), ())), preferred_element_type=jnp.float32)
        return total[0:8] + total[8:16] + total[16:24]

    def overlay():
        lane = iota((CY, 128), 1)
        for x in range(CX):
            rows = nst[LAM0, (1 + x // 8) * WY + 8:(1 + x // 8) * WY + 8 + CY]
            j = x % 8
            rows = pltpu.roll(rows, 128 - 16 * j, axis=1) if j else rows
            adj_ref[x, :, 0:128] = jnp.where(lane < 5, rows, adj_ref[x, :, 0:128])

    zero_edges()
    table = swap(table_ref[...].astype(jnp.float32))
    pl.semaphore_wait(barrier, NG - 1 + NB - 1 + len(corners))
    first = stage_one(table)
    for i, f in ((0, T0), (1, DD), (2, L3)):
        for load in edge_loads[i]:
            load.wait()
        loads[i].wait()
        if f != L3:
            send(f)
    conduct(0, T0)
    conduct_own(0, T0)
    second = stage_two(first)
    top_pack()
    tops = top_copies()
    send(L3)
    forward(0, T0, T1)
    arrive(T0)
    arrive(DD)
    conduct_halo(0, T0)
    forward_faces(0, T0, T1)
    add_delta(T1)
    send(T1)
    for sends, _, c in tops:
        when(sends, c.start)
    patches = split3(patch_ref[...])

    spot = finish(second).astype(jnp.int32)
    p_high = spot >> 7
    make_hot(hot_p, spot & 127)
    post(0, neighbours(lookup(patches, hot_p, p_high, 64)))

    conduct(1, T1)
    conduct_own(1, T1)
    forward(1, T1, T2)

    arrive(T1)
    conduct_halo(1, T1)
    forward_faces(1, T1, T2)
    add_delta(T2)
    send(T2)

    for _, receives, c in tops:
        when(receives, c.wait_recv)
    def whole(i):
        return top[i].reshape(TR, 128)
    t0, d, l3 = in_grid(whole(0)), in_grid(whole(1)), in_grid(whole(2))
    entry = to_lines(whole(3)).astype(jnp.int32)
    top_hot(entry)
    k0, s0 = top_conduct(t0, d)
    nst[KAY0], nst[SLP0] = k0, s0
    nst[TEM1] = top_forward(t0, k0)

    conduct(2, T2)
    conduct_own(2, T2)
    reverse(2, T2, L3, L2)
    arrive(L3)
    arrive(T2)
    conduct_halo(2, T2)
    reverse_faces(2, T2, L3, L2)
    add_delta(L2)
    send(L2)
    heat = SOURCE * top_heat(collect(0, 72), entry)
    t1 = in_grid(nst[TEM1] + heat)
    k1, s1 = top_conduct(t1, d)
    t2 = in_grid(top_forward(t1, k1) + heat)
    k2, s2 = top_conduct(t2, d)
    l2 = top_reverse(t2, k2, s2, l3)
    l1 = top_reverse(t1, k1, s1, l2)
    post(1, top_slots(SOURCE * (l3 + l2 + l1), entry))
    nst[LAM1] = l1

    nst[LAM0] = top_reverse(in_grid(whole(0)), nst[KAY0], nst[SLP0], nst[LAM1])
    reverse(1, T1, L2, L1)
    arrive(L2)
    reverse_faces(1, T1, L2, L1)
    add_delta(L1)
    send(L1)
    reverse(0, T0, L1, None)
    flux_ref[...] = scatter(collect(1, 8), hot_p, p_high, 64)
    arrive(L1)
    reverse_faces(0, T0, L1, None)
    add_delta(None)
    overlay()

    for n in range(2):
        everything(n).wait_send()
    for c in first + second:
        c.wait_send()
    for f in range(7):
        sent(f)
    for sends, _, c in tops:
        when(sends, c.wait_send)


def shards(state, diffusivity, patches, entries, table, sensitivity):
    anywhere = pl.BlockSpec(memory_space=pl.ANY)
    vmem = pl.BlockSpec(memory_space=pltpu.VMEM)
    f32, bf16 = jnp.float32, jnp.bfloat16
    flux, adjoint = pl.pallas_call(
        kernel,
        out_shape=(
            jax.ShapeDtypeStruct((64, 128), f32),
            jax.ShapeDtypeStruct((CX, CY, CZ), f32),
        ),
        in_specs=[anywhere, anywhere, anywhere, vmem, vmem, vmem],
        out_specs=(vmem, vmem),
        scratch_shapes=[
            pltpu.VMEM((7, CX + 2, CY, CZ), f32),
            pltpu.VMEM((3, CX + 2, CY, CZ), f32),
            pltpu.VMEM((3, CX + 2, CY, CZ), f32),
            pltpu.VMEM((7, 2, CX, CZ), f32),
            pltpu.VMEM((7, 2, CX, CZ), f32),
            pltpu.VMEM((3, 2, CX, CZ), f32),
            pltpu.VMEM((3, 2, CX, CZ), f32),
            pltpu.VMEM((3, 2, CX, CZ), f32),
            pltpu.VMEM((2, CX, CZ), f32),
            pltpu.VMEM((2, NG * NB, 128), f32),
            pltpu.VMEM((2, NG * NB, 128), f32),
            pltpu.VMEM((2, 8, 128), f32),
            pltpu.VMEM((NB, 8, 128), f32),
            pltpu.VMEM((128, 8 * TL), bf16),
            pltpu.VMEM((128, 1024), bf16),
            pltpu.VMEM((4, 6, WY, 128), f32),
            pltpu.VMEM((5, TR, 128), f32),
            pltpu.VMEM((128, TL), f32),
            pltpu.SemaphoreType.DMA((3, 3)),
            pltpu.SemaphoreType.DMA((7, 4)),
            pltpu.SemaphoreType.DMA((7, 4)),
            pltpu.SemaphoreType.DMA((3,)),
            pltpu.SemaphoreType.DMA((3,)),
            pltpu.SemaphoreType.DMA((NG,)),
            pltpu.SemaphoreType.DMA((NG,)),
            pltpu.SemaphoreType.DMA((NB,)),
            pltpu.SemaphoreType.DMA((NB,)),
            pltpu.SemaphoreType.DMA((9,)),
            pltpu.SemaphoreType.DMA((9,)),
        ],
        compiler_params=pltpu.CompilerParams(
            collective_id=0, has_side_effects=True, vmem_limit_bytes=52 * 1024 * 1024),
    )(
        state, diffusivity, sensitivity, patches.reshape(64, 128),
        entries, jnp.swapaxes(table[0], 0, 1),
    )
    return flux.reshape(-1), adjoint


def solution(mesh):
    return jax.shard_map(
        shards,
        mesh=mesh,
        in_specs=(
            P("gx", "bulk", None),
            P("gx", "bulk", None),
            P(("gx", "bulk")),
            P("gx", "bulk"),
            P(("gx", "bulk"), None, None),
            P("gx", "bulk", None),
        ),
        out_specs=(P(("gx", "bulk")), P("gx", "bulk", None)),
        check_vma=False,
    )
```

```python
import jax
import jax.numpy as jnp
from jax import lax
from jax.experimental import pallas as pl
from jax.experimental.pallas import tpu as pltpu
from jax.sharding import PartitionSpec as P

MESH = pl.DeviceIdType.MESH
RATE = 0.08
DRIFT = 0.2
SOURCE = 0.5
HALF_RATE = 0.5 * RATE

NG, NB = 8, 16
CX, CY, CZ = 32, 32, 256

T0, DD, L3, T1, T2, L2, L1 = range(7)

WY = CY + 16
TR = 6 * WY
TL = 384
KAY0, SLP0, TEM1, LAM1, LAM0 = range(5)


def split3(x):
    hi = x.astype(jnp.bfloat16)
    rest = x - hi.astype(jnp.float32)
    mid = rest.astype(jnp.bfloat16)
    low = (rest - mid.astype(jnp.float32)).astype(jnp.bfloat16)
    return hi, mid, low


def iota(shape, axis):
    return lax.broadcasted_iota(jnp.int32, shape, axis)


def kernel(
    t0_hbm, d_hbm, l3_hbm, patch_ref, entry_ref, table_ref,
    flux_ref, adj_ref,
    fld, kay, slp, yrecv, ysend, kyh, kyf, syf, delta, outbox, inbox, rows, gath, hot_n, hot_p, top, nst, turn,
    load_sem, xs_sem, xr_sem, a_send, a_recv, g_send, g_recv, b_send, b_recv, t_send, t_recv,
):
    g = lax.axis_index("gx")
    b = lax.axis_index("bulk")
    me = g * NB + b

    inputs = ((T0, t0_hbm), (DD, d_hbm), (L3, l3_hbm))
    edge_loads = [
        [pltpu.make_async_copy(src.at[:, y, :], ysend.at[f, side], load_sem.at[f, side])
         for side, y in ((0, 0), (1, CY - 1))]
        for f, src in inputs
    ]
    loads = [
        pltpu.make_async_copy(src, fld.at[f, pl.ds(1, CX)], load_sem.at[f, 2])
        for f, src in inputs
    ]
    for pair in edge_loads:
        for load in pair:
            load.start()
    for load in loads:
        load.start()
    barrier = pltpu.get_barrier_semaphore()

    def each_other(act):
        for j in range(1, NB):
            act(g, ((b + j) & (NB - 1)))

        def body(i, _):
            for j in range(NB):
                act(((g + i) & (NG - 1)), ((b + j) & (NB - 1)))
            return 0
        lax.fori_loop(1, NG, body, 0)

    for k in range(1, NG):
        pl.semaphore_signal(barrier, inc=1, device_id=(((g + k) & (NG - 1)), b), device_id_type=MESH)
    for k in range(1, NB):
        pl.semaphore_signal(barrier, inc=1, device_id=(g, ((b + k) & (NB - 1))), device_id_type=MESH)
    corners = [(i, j) for i in (1, NG - 1) for j in (1, NB - 1)]
    for i, j in corners:
        pl.semaphore_signal(
            barrier, inc=1, device_id=(((g + i) & (NG - 1)), ((b + j) & (NB - 1))), device_id_type=MESH)

    def swap(a):
        lane, sub = iota((8, 128), 1), iota((8, 128), 0)
        out = jnp.zeros((8, 128), jnp.float32)
        for k in range(8):
            turned = pltpu.roll(a, 16 * k, axis=1) if k else a
            kept = jnp.where((lane >> 4) == sub, turned, 0.0)
            out = out + (pltpu.roll(kept, 8 - k, axis=0) if k else kept)
        return out

    def stage_one(block):
        rows[0] = block
        rows[1, pl.ds(g, 1)] = rows[0, pl.ds(g, 1)]
        copies = []
        for k in range(1, NG):
            o = ((g + k) & (NG - 1))
            c = pltpu.make_async_remote_copy(
                src_ref=rows.at[0, pl.ds(o, 1)], dst_ref=rows.at[1, pl.ds(g, 1)],
                send_sem=g_send.at[k], recv_sem=g_recv.at[k],
                device_id=(o, b), device_id_type=MESH)
            c.start()
            copies.append(c)
        return copies

    def stage_two(first):
        for c in first:
            c.wait_recv()
        copies = []
        for k in range(1, NB):
            c = pltpu.make_async_remote_copy(
                src_ref=rows.at[1], dst_ref=gath.at[b],
                send_sem=b_send.at[k], recv_sem=b_recv.at[k],
                device_id=(g, ((b + k) & (NB - 1))), device_id_type=MESH)
            c.start()
            copies.append(c)
        gath[b] = rows[1]
        return copies

    def finish(second):
        for c in second:
            c.wait_recv()
        lane = iota((8, 128), 1)
        out = jnp.zeros((8, 128), jnp.float32)
        for k in range(NB):
            turned = pltpu.roll(gath[k], lax.rem(k - b + 128, 128), axis=1)
            out = out + jnp.where((lane & 15) == k, turned, 0.0)
        return swap(out)

    def post(n, block):
        pad = jnp.zeros((128 - block.shape[0], 128), jnp.float32)
        outbox[n] = jnp.concatenate([block, pad], axis=0).T

        def act(tg, tb):
            pltpu.make_async_remote_copy(
                src_ref=outbox.at[n, pl.ds(tg * NB + tb, 1)], dst_ref=inbox.at[n, pl.ds(me, 1)],
                send_sem=a_send.at[n], recv_sem=a_recv.at[n],
                device_id=(tg, tb), device_id_type=MESH).start()
        each_other(act)
        inbox[n, pl.ds(me, 1)] = outbox[n, pl.ds(me, 1)]

    def everything(n):
        return pltpu.make_async_remote_copy(
            src_ref=outbox.at[n, pl.ds(0, NG * NB - 1)], dst_ref=inbox.at[n, pl.ds(0, NG * NB - 1)],
            send_sem=a_send.at[n], recv_sem=a_recv.at[n],
            device_id=(g, b), device_id_type=MESH)

    def collect(n, count):
        everything(n).wait_recv()
        return inbox[n].T[0:count]

    def make_hot(hot, low):
        for q in range(8):
            hit = iota((128, 128), 0) == low[q:q + 1, :]
            hot[:, q * 128:(q + 1) * 128] = jnp.where(hit, 1.0, 0.0).astype(jnp.bfloat16)

    def lookup(parts, hot, high, count):
        stacked = jnp.concatenate(parts, axis=0)
        found = jnp.dot(stacked, hot[...], preferred_element_type=jnp.float32)
        total = found[:count] + found[count:2 * count] + found[2 * count:]
        out = []
        for q in range(8):
            piece = total[:, q * 128:(q + 1) * 128]
            hit = iota((count, 128), 0) == high[q:q + 1, :]
            out.append(jnp.sum(jnp.where(hit, piece, 0.0), axis=0, keepdims=True))
        return jnp.concatenate(out, axis=0)

    def scatter(values, hot, high, count):
        spread = jnp.concatenate(
            [jnp.where(iota((count, 128), 0) == high[q:q + 1, :], values[q:q + 1, :], 0.0)
             for q in range(8)], axis=1)
        total = jnp.zeros((count, 128), jnp.float32)
        for part in split3(spread):
            total = total + lax.dot_general(
                part, hot[...], (((1,), (1,)), ((), ())), preferred_element_type=jnp.float32)
        return total

    def zero_edges():
        for edge, plane, side in ((g == 0, 0, None), (g == NG - 1, CX + 1, None),
                                  (b == 0, None, 0), (b == NB - 1, None, 1)):
            @pl.when(edge)
            def _():
                for f in range(7):
                    if plane is not None:
                        fld[f, plane] = jnp.zeros((CY, CZ), jnp.float32)
                    else:
                        yrecv[f, side] = jnp.zeros((CX, CZ), jnp.float32)

    def faces(f):
        def remote(src, dst, way, target):
            return pltpu.make_async_remote_copy(
                src_ref=src, dst_ref=dst, send_sem=xs_sem.at[f, way], recv_sem=xr_sem.at[f, way],
                device_id=target, device_id_type=MESH)
        return (
            (g > 0, g < NG - 1, remote(fld.at[f, 1], fld.at[f, CX + 1], 0, (lax.max(g - 1, 0), b))),
            (g < NG - 1, g > 0, remote(fld.at[f, CX], fld.at[f, 0], 1, (lax.min(g + 1, NG - 1), b))),
            (b > 0, b < NB - 1, remote(ysend.at[f, 0], yrecv.at[f, 1], 2, (g, lax.max(b - 1, 0)))),
            (b < NB - 1, b > 0, remote(ysend.at[f, 1], yrecv.at[f, 0], 3, (g, lax.min(b + 1, NB - 1)))),
        )

    def send(f):
        for sends, _, c in faces(f):
            @pl.when(sends)
            def _():
                c.start()

    def arrive(f):
        for _, receives, c in faces(f):
            @pl.when(receives)
            def _():
                c.wait_recv()

    def sent(f):
        for sends, _, c in faces(f):
            @pl.when(sends)
            def _():
                c.wait_send()

    row = iota((CY, CZ), 0)
    col = iota((CY, CZ), 1)

    def y_down(a):
        return pltpu.roll(a, 1, axis=0)

    def y_up(a):
        return pltpu.roll(a, CY - 1, axis=0)

    def k_down(a):
        return pltpu.roll(a, 1, axis=1)

    def k_up(a):
        return pltpu.roll(a, CZ - 1, axis=1)

    def planes(step, carry):
        carry = lax.fori_loop(1, CX - 3, lambda x, c: step(x, c, False), carry, unroll=4)
        for x in range(CX - 3, CX + 1):
            carry = step(x, carry, x == CX)

    def conduct(n, f):
        def body(x, _):
            h = jnp.tanh(fld[f, x])
            d = fld[DD, x] * HALF_RATE
            kay[n, x] = d + (0.5 * d) * h
            slp[n, x] = (0.5 * d) * (1.0 - h * h)
            return 0
        lax.fori_loop(1, CX + 1, body, 0, unroll=4)

    def conduct_own(n, f):
        for side in range(2):
            h = jnp.tanh(ysend[f, side])
            d = ysend[DD, side] * HALF_RATE
            kyf[n, side] = d + (0.5 * d) * h
            syf[n, side] = (0.5 * d) * (1.0 - h * h)

    def conduct_halo(n, f):
        for x in (0, CX + 1):
            kay[n, x] = HALF_RATE * fld[DD, x] * (1.0 + 0.5 * jnp.tanh(fld[f, x]))
        for side in range(2):
            kyh[n, side] = HALF_RATE * yrecv[DD, side] * (1.0 + 0.5 * jnp.tanh(yrecv[f, side]))

    def forward(n, f, out):
        def step(x, flow_low, last):
            t, k = fld[f, x], kay[n, x]
            acc = (1.0 - DRIFT) * t - flow_low[0] + flow_low[1]
            flow = None
            if not last:
                flow = (k + kay[n, x + 1]) * (fld[f, x + 1] - t)
                acc = acc + flow
            y_l = jnp.where(row == 0, 0.0, (k + y_down(k)) * (t - y_down(t)))
            acc = acc + (y_up(y_l) - y_l)
            kt = k * t
            k_l = jnp.where(col == 0, kt, (k + k_down(k)) * (t - k_down(t)))
            acc = acc + (jnp.where(col == CZ - 1, -kt, k_up(k_l)) - k_l)
            fld[out, x] = acc
            return flow, DRIFT * t
        zero = jnp.zeros((CY, CZ), jnp.float32)
        planes(step, (zero, zero))

    def forward_faces(n, f, out):
        low, high = fld[f, 0], fld[f, CX + 1]
        fld[out, 1] = fld[out, 1] + DRIFT * low - (kay[n, 0] + kay[n, 1]) * (fld[f, 1] - low)
        fld[out, CX] = fld[out, CX] + (kay[n, CX] + kay[n, CX + 1]) * (high - fld[f, CX])
        for side in range(2):
            delta[side] = (kyf[n, side] + kyh[n, side]) * (yrecv[f, side] - ysend[f, side])

    def reverse(n, f, lam, out):
        def step(x, carry, last):
            g_x, m_x = carry
            t, k, l = fld[f, x], kay[n, x], fld[lam, x]
            bend = g_x
            acc = (1.0 - DRIFT) * l + m_x
            g_u = m_u = None
            if not last:
                l_up = fld[lam, x + 1]
                w = l - l_up
                g_u = w * (fld[f, x + 1] - t)
                m_u = w * (k + kay[n, x + 1])
                bend = bend + g_u
                acc = acc + (DRIFT * l_up - m_u)
            w = jnp.where(row == 0, 0.0, y_down(l) - l)
            g_l = w * (t - y_down(t))
            m_l = w * (k + y_down(k))
            bend = bend + (g_l + y_up(g_l))
            acc = acc + (m_l - y_up(m_l))
            lt, lk = l * t, l * k
            w = k_down(l) - l
            g_l = jnp.where(col == 0, -lt, w * (t - k_down(t)))
            m_l = jnp.where(col == 0, -lk, w * (k + k_down(k)))
            bend = bend + (g_l + jnp.where(col == CZ - 1, -lt, k_up(g_l)))
            acc = acc + (m_l - jnp.where(col == CZ - 1, lk, k_up(m_l)))
            value = acc + slp[n, x] * bend
            if out is None:
                adj_ref[x - 1] = value
            else:
                fld[out, x] = value
            return g_u, m_u
        zero = jnp.zeros((CY, CZ), jnp.float32)
        planes(step, (zero, zero))

    def reverse_faces(n, f, lam, out):
        w = fld[lam, 0] - fld[lam, 1]
        low = (slp[n, 1] * (w * (fld[f, 1] - fld[f, 0])) + w * (kay[n, 0] + kay[n, 1]))
        w = fld[lam, CX] - fld[lam, CX + 1]
        high = (slp[n, CX] * (w * (fld[f, CX + 1] - fld[f, CX])) - w * (kay[n, CX] + kay[n, CX + 1])
                + DRIFT * fld[lam, CX + 1])
        if out is None:
            adj_ref[0] = adj_ref[0] + low
            adj_ref[CX - 1] = adj_ref[CX - 1] + high
        else:
            fld[out, 1] = fld[out, 1] + low
            fld[out, CX] = fld[out, CX] + high
        for side in range(2):
            w = yrecv[lam, side] - ysend[lam, side]
            bend = w * (ysend[f, side] - yrecv[f, side])
            delta[side] = syf[n, side] * bend + w * (kyf[n, side] + kyh[n, side])

    def add_delta(f):
        def body(x, _):
            for side, y in ((0, slice(0, 1)), (1, slice(CY - 1, CY))):
                if f is None:
                    adj_ref[x, y] = adj_ref[x, y] + delta[side, pl.ds(x, 1), :]
                else:
                    new = fld[f, x + 1, y] + delta[side, pl.ds(x, 1), :]
                    fld[f, x + 1, y] = new
                    ysend[f, side, pl.ds(x, 1), :] = new
            return 0
        lax.fori_loop(0, CX, body, 0, unroll=4)

    wide = iota((TR, 128), 1)
    tall = iota((TR, 128), 0)
    strip = (tall * 1366) >> 16
    inside = tall - WY * strip
    outside = (
        ((strip == 0) & (g == 0)) | ((strip == 5) & (g == NG - 1))
        | ((inside < 8) & (b == 0)) | ((inside >= 8 + CY) & (b == NB - 1))
    )
    surface = (wide & 15) == 0

    def in_grid(a):
        return jnp.where(outside, 0.0, a)

    def next_x(a):
        r = pltpu.roll(a, 112, axis=1)
        return jnp.where(wide < 112, r, jnp.concatenate([r[WY:], r[:WY]], axis=0))

    def last_x(a):
        r = pltpu.roll(a, 16, axis=1)
        return jnp.where(wide >= 16, r, jnp.concatenate([r[TR - WY:], r[:TR - WY]], axis=0))

    def next_y(a):
        return pltpu.roll(a, TR - 1, axis=0)

    def last_y(a):
        return pltpu.roll(a, 1, axis=0)

    def next_k(a):
        return pltpu.roll(a, 127, axis=1)

    def last_k(a):
        return pltpu.roll(a, 1, axis=1)

    def top_conduct(t, d):
        h = jnp.tanh(t)
        d = d * HALF_RATE
        return d + (0.5 * d) * h, (0.5 * d) * (1.0 - h * h)

    def top_forward(t, k):
        flow = (k + next_x(k)) * (next_x(t) - t)
        acc = (1.0 - DRIFT) * t + DRIFT * last_x(t) + (flow - last_x(flow))
        flow = (k + next_y(k)) * (next_y(t) - t)
        acc = acc + (flow - last_y(flow))
        flow = jnp.where(surface, k * t, (k + last_k(k)) * (t - last_k(t)))
        return acc + (next_k(flow) - flow)

    def top_reverse(t, k, s, l):
        l_up = next_x(l)
        w = l - l_up
        bent = w * (next_x(t) - t)
        moved = w * (k + next_x(k))
        bend = bent + last_x(bent)
        acc = (1.0 - DRIFT) * l + DRIFT * l_up + (last_x(moved) - moved)
        w = l - next_y(l)
        bent = w * (next_y(t) - t)
        moved = w * (k + next_y(k))
        bend = bend + (bent + last_y(bent))
        acc = acc + (last_y(moved) - moved)
        w = last_k(l) - l
        bent = jnp.where(surface, -(l * t), w * (t - last_k(t)))
        moved = jnp.where(surface, -(l * k), w * (k + last_k(k)))
        bend = bend + (bent + next_k(bent))
        acc = acc + (moved - next_k(moved))
        return in_grid(acc + s * bend)

    def top_pack():
        lane = iota((CY, 128), 1) >> 4
        for i, f in enumerate((T0, DD, L3)):
            for strip_x in range(4):
                x = 1 + 8 * strip_x
                tile = fld[f, x, :, 0:128]
                for j in range(1, 8):
                    tile = jnp.where(lane == j, pltpu.roll(fld[f, x + j, :, 0:128], 16 * j, axis=1), tile)
                top[i, 1 + strip_x, 8:8 + CY] = tile
        entry = jnp.concatenate([entry_ref[...], jnp.zeros((CX, 128 - CY), jnp.int32)], axis=1)
        entry = jnp.concatenate([entry.astype(jnp.float32), jnp.zeros((128 - CX, 128), jnp.float32)], axis=0)
        entry = entry.T[0:CY].astype(jnp.int32)
        spread = jnp.where(iota((128, 512), 0) == (iota((128, 512), 1) >> 4), 1.0, 0.0).astype(jnp.bfloat16)
        high = jnp.dot((entry >> 3).astype(jnp.float32).astype(jnp.bfloat16), spread,
                       preferred_element_type=jnp.float32)
        low = jnp.dot((entry & 7).astype(jnp.float32).astype(jnp.bfloat16), spread,
                      preferred_element_type=jnp.float32)
        entry = 8.0 * high + low
        for strip_x in range(4):
            top[3, 1 + strip_x, 8:8 + CY] = entry[:, 128 * strip_x:128 * (strip_x + 1)]

    def top_copies():
        out = []
        along_x = {-1: (1, 1, 5), 0: (1, 4, 1), 1: (4, 1, 0)}
        along_y = {-1: (8, 8, 8 + CY), 0: (8, CY, 8), 1: (CY, 8, 0)}
        for dx in (-1, 0, 1):
            for dy in (-1, 0, 1):
                if dx == 0 and dy == 0:
                    continue
                way = (dx + 1) * 3 + dy + 1
                x, wide_x, to_x = along_x[dx]
                y, wide_y, to_y = along_y[dy]
                sends, receives = None, None
                for d, at, size in ((dx, g, NG), (dy, b, NB)):
                    if d:
                        one = (at > 0, at < size - 1)
                        one = one if d < 0 else one[::-1]
                        sends = one[0] if sends is None else sends & one[0]
                        receives = one[1] if receives is None else receives & one[1]
                target = (lax.clamp(0, g + dx, NG - 1), lax.clamp(0, b + dy, NB - 1))
                out.append((sends, receives, pltpu.make_async_remote_copy(
                    src_ref=top.at[:, pl.ds(x, wide_x), pl.ds(y, wide_y)],
                    dst_ref=top.at[:, pl.ds(to_x, wide_x), pl.ds(to_y, wide_y)],
                    send_sem=t_send.at[way], recv_sem=t_recv.at[way],
                    device_id=target, device_id_type=MESH)))
        return out

    def when(condition, action):
        @pl.when(condition)
        def _():
            action()

    line = iota((1, TL), 1)
    line_strip = (line * 1366) >> 16
    line_y = line - WY * line_strip
    side_x = jnp.where(line_strip == 0, 0, jnp.where(line_strip >= 5, 2, 1))
    side_y = jnp.where(line_y < 8, 0, jnp.where(line_y >= 8 + CY, 2, 1))
    whose = 3 * side_x + side_y
    ours = whose == 4

    def to_lines(a):
        turned = jnp.concatenate([a, jnp.zeros((TL - TR, 128), jnp.float32)], axis=0).T
        return jnp.concatenate([turned[16 * j:16 * j + 1] for j in range(8)], axis=0)

    def from_lines(lines):
        turn[...] = jnp.zeros((128, TL), jnp.float32)
        for j in range(8):
            turn[16 * j:16 * j + 1, :] = lines[j]
        return turn[...].T[0:TR]

    def neighbours(v):
        return jnp.concatenate(
            [pltpu.roll(v, (-(NB * dx + dy)) % 128, axis=1) if dx or dy else v
             for dx in (-1, 0, 1) for dy in (-1, 0, 1)], axis=0)

    def top_hot(entry):
        for j in range(8):
            hit = iota((128, TL), 0) == (entry[j:j + 1] >> 3)
            hot_n[:, j * TL:(j + 1) * TL] = jnp.where(hit, 1.0, 0.0).astype(jnp.bfloat16)

    def top_heat(slots, entry):
        stacked = jnp.concatenate(split3(slots), axis=0)
        lines = []
        for j in range(8):
            found = jnp.dot(stacked, hot_n[:, j * TL:(j + 1) * TL], preferred_element_type=jnp.float32)
            found = found[:72] + found[72:144] + found[144:]
            hit = iota((72, TL), 0) == 8 * whose + (entry[j:j + 1] & 7)
            lines.append(jnp.sum(jnp.where(hit, found, 0.0), axis=0, keepdims=True))
        return from_lines(lines)

    def top_slots(a, entry):
        lines = to_lines(a)
        spread = jnp.concatenate(
            [jnp.where((iota((8, TL), 0) == (entry[j:j + 1] & 7)) & ours, lines[j:j + 1], 0.0)
             for j in range(8)], axis=1)
        stacked = jnp.concatenate(split3(spread), axis=0)
        total = lax.dot_general(
            stacked, hot_n[...], (((1,), (1,)), ((), ())), preferred_element_type=jnp.float32)
        return total[0:8] + total[8:16] + total[16:24]

    def overlay():
        lane = iota((CY, 128), 1)
        for x in range(CX):
            rows = nst[LAM0, (1 + x // 8) * WY + 8:(1 + x // 8) * WY + 8 + CY]
            j = x % 8
            rows = pltpu.roll(rows, 128 - 16 * j, axis=1) if j else rows
            adj_ref[x, :, 0:128] = jnp.where(lane < 5, rows, adj_ref[x, :, 0:128])

    zero_edges()
    table = swap(table_ref[...].astype(jnp.float32))
    pl.semaphore_wait(barrier, NG - 1 + NB - 1 + len(corners))
    first = stage_one(table)
    for i, f in ((0, T0), (1, DD), (2, L3)):
        for load in edge_loads[i]:
            load.wait()
        loads[i].wait()
        if f != L3:
            send(f)
    conduct(0, T0)
    conduct_own(0, T0)
    top_pack()
    tops = top_copies()
    send(L3)
    forward(0, T0, T1)
    second = stage_two(first)
    arrive(T0)
    arrive(DD)
    conduct_halo(0, T0)
    forward_faces(0, T0, T1)
    add_delta(T1)
    send(T1)
    for sends, _, c in tops:
        when(sends, c.start)
    patches = split3(patch_ref[...])

    spot = finish(second).astype(jnp.int32)
    p_high = spot >> 7
    make_hot(hot_p, spot & 127)
    post(0, neighbours(lookup(patches, hot_p, p_high, 64)))

    conduct(1, T1)
    conduct_own(1, T1)
    forward(1, T1, T2)

    arrive(T1)
    conduct_halo(1, T1)
    forward_faces(1, T1, T2)
    add_delta(T2)
    send(T2)

    for _, receives, c in tops:
        when(receives, c.wait_recv)
    def whole(i):
        return top[i].reshape(TR, 128)
    t0, d, l3 = in_grid(whole(0)), in_grid(whole(1)), in_grid(whole(2))
    entry = to_lines(whole(3)).astype(jnp.int32)
    top_hot(entry)
    k0, s0 = top_conduct(t0, d)
    nst[KAY0], nst[SLP0] = k0, s0
    nst[TEM1] = top_forward(t0, k0)

    conduct(2, T2)
    conduct_own(2, T2)
    reverse(2, T2, L3, L2)
    arrive(L3)
    arrive(T2)
    conduct_halo(2, T2)
    reverse_faces(2, T2, L3, L2)
    add_delta(L2)
    send(L2)
    heat = SOURCE * top_heat(collect(0, 72), entry)
    t1 = in_grid(nst[TEM1] + heat)
    k1, s1 = top_conduct(t1, d)
    t2 = in_grid(top_forward(t1, k1) + heat)
    k2, s2 = top_conduct(t2, d)
    l2 = top_reverse(t2, k2, s2, l3)
    l1 = top_reverse(t1, k1, s1, l2)
    post(1, top_slots(SOURCE * (l3 + l2 + l1), entry))
    nst[LAM1] = l1

    reverse(1, T1, L2, L1)
    arrive(L2)
    reverse_faces(1, T1, L2, L1)
    add_delta(L1)
    send(L1)
    nst[LAM0] = top_reverse(in_grid(whole(0)), nst[KAY0], nst[SLP0], nst[LAM1])
    reverse(0, T0, L1, None)
    flux_ref[...] = scatter(collect(1, 8), hot_p, p_high, 64)
    arrive(L1)
    reverse_faces(0, T0, L1, None)
    add_delta(None)
    overlay()

    for n in range(2):
        everything(n).wait_send()
    for c in first + second:
        c.wait_send()
    for f in range(7):
        sent(f)
    for sends, _, c in tops:
        when(sends, c.wait_send)


def shards(state, diffusivity, patches, entries, table, sensitivity):
    anywhere = pl.BlockSpec(memory_space=pl.ANY)
    vmem = pl.BlockSpec(memory_space=pltpu.VMEM)
    f32, bf16 = jnp.float32, jnp.bfloat16
    flux, adjoint = pl.pallas_call(
        kernel,
        out_shape=(
            jax.ShapeDtypeStruct((64, 128), f32),
            jax.ShapeDtypeStruct((CX, CY, CZ), f32),
        ),
        in_specs=[anywhere, anywhere, anywhere, vmem, vmem, vmem],
        out_specs=(vmem, vmem),
        scratch_shapes=[
            pltpu.VMEM((7, CX + 2, CY, CZ), f32),
            pltpu.VMEM((3, CX + 2, CY, CZ), f32),
            pltpu.VMEM((3, CX + 2, CY, CZ), f32),
            pltpu.VMEM((7, 2, CX, CZ), f32),
            pltpu.VMEM((7, 2, CX, CZ), f32),
            pltpu.VMEM((3, 2, CX, CZ), f32),
            pltpu.VMEM((3, 2, CX, CZ), f32),
            pltpu.VMEM((3, 2, CX, CZ), f32),
            pltpu.VMEM((2, CX, CZ), f32),
            pltpu.VMEM((2, NG * NB, 128), f32),
            pltpu.VMEM((2, NG * NB, 128), f32),
            pltpu.VMEM((2, 8, 128), f32),
            pltpu.VMEM((NB, 8, 128), f32),
            pltpu.VMEM((128, 8 * TL), bf16),
            pltpu.VMEM((128, 1024), bf16),
            pltpu.VMEM((4, 6, WY, 128), f32),
            pltpu.VMEM((5, TR, 128), f32),
            pltpu.VMEM((128, TL), f32),
            pltpu.SemaphoreType.DMA((3, 3)),
            pltpu.SemaphoreType.DMA((7, 4)),
            pltpu.SemaphoreType.DMA((7, 4)),
            pltpu.SemaphoreType.DMA((3,)),
            pltpu.SemaphoreType.DMA((3,)),
            pltpu.SemaphoreType.DMA((NG,)),
            pltpu.SemaphoreType.DMA((NG,)),
            pltpu.SemaphoreType.DMA((NB,)),
            pltpu.SemaphoreType.DMA((NB,)),
            pltpu.SemaphoreType.DMA((9,)),
            pltpu.SemaphoreType.DMA((9,)),
        ],
        compiler_params=pltpu.CompilerParams(
            collective_id=0, has_side_effects=True, vmem_limit_bytes=52 * 1024 * 1024),
    )(
        state, diffusivity, sensitivity, patches.reshape(64, 128),
        entries, jnp.swapaxes(table[0], 0, 1),
    )
    return flux.reshape(-1), adjoint


def solution(mesh):
    return jax.shard_map(
        shards,
        mesh=mesh,
        in_specs=(
            P("gx", "bulk", None),
            P("gx", "bulk", None),
            P(("gx", "bulk")),
            P("gx", "bulk"),
            P(("gx", "bulk"), None, None),
            P("gx", "bulk", None),
        ),
        out_specs=(P(("gx", "bulk")), P("gx", "bulk", None)),
        check_vma=False,
    )
```

```python
import jax
import jax.numpy as jnp
from jax import lax
from jax.experimental import pallas as pl
from jax.experimental.pallas import tpu as pltpu
from jax.sharding import PartitionSpec as P

MESH = pl.DeviceIdType.MESH
RATE = 0.08
DRIFT = 0.2
SOURCE = 0.5
HALF_RATE = 0.5 * RATE

NG, NB = 8, 16
CX, CY, CZ = 32, 32, 256

T0, DD, L3, T1, T2, L2, L1 = range(7)

WY = CY + 16
TR = 6 * WY
TL = 384
KAY0, SLP0, TEM1, LAM1, LAM0 = range(5)


def split3(x):
    hi = x.astype(jnp.bfloat16)
    rest = x - hi.astype(jnp.float32)
    mid = rest.astype(jnp.bfloat16)
    low = (rest - mid.astype(jnp.float32)).astype(jnp.bfloat16)
    return hi, mid, low


def iota(shape, axis):
    return lax.broadcasted_iota(jnp.int32, shape, axis)


def kernel(
    t0_hbm, d_hbm, l3_hbm, patch_ref, entry_ref, table_ref,
    flux_ref, adj_ref,
    fld, kay, slp, yrecv, ysend, kyh, kyf, syf, delta, outbox, inbox, rows, gath, hot_n, hot_p, top, nst, turn,
    load_sem, xs_sem, xr_sem, a_send, a_recv, g_send, g_recv, b_send, b_recv, t_send, t_recv,
):
    g = lax.axis_index("gx")
    b = lax.axis_index("bulk")
    me = g * NB + b

    inputs = ((T0, t0_hbm), (DD, d_hbm), (L3, l3_hbm))
    edge_loads = [
        [pltpu.make_async_copy(src.at[:, y, :], ysend.at[f, side], load_sem.at[f, side])
         for side, y in ((0, 0), (1, CY - 1))]
        for f, src in inputs
    ]
    loads = [
        pltpu.make_async_copy(src, fld.at[f, pl.ds(1, CX)], load_sem.at[f, 2])
        for f, src in inputs
    ]
    barrier = pltpu.get_barrier_semaphore()

    def each_other(act):
        for j in range(1, NB):
            act(g, ((b + j) & (NB - 1)))

        def body(i, _):
            for j in range(NB):
                act(((g + i) & (NG - 1)), ((b + j) & (NB - 1)))
            return 0
        lax.fori_loop(1, NG, body, 0)

    for k in range(1, NG):
        pl.semaphore_signal(barrier, inc=1, device_id=(((g + k) & (NG - 1)), b), device_id_type=MESH)
    for k in range(1, NB):
        pl.semaphore_signal(barrier, inc=1, device_id=(g, ((b + k) & (NB - 1))), device_id_type=MESH)
    corners = [(i, j) for i in (1, NG - 1) for j in (1, NB - 1)]
    for i, j in corners:
        pl.semaphore_signal(
            barrier, inc=1, device_id=(((g + i) & (NG - 1)), ((b + j) & (NB - 1))), device_id_type=MESH)

    for pair in edge_loads:
        for load in pair:
            load.start()
    for load in loads:
        load.start()

    def swap(a):
        lane, sub = iota((8, 128), 1), iota((8, 128), 0)
        out = jnp.zeros((8, 128), jnp.float32)
        for k in range(8):
            turned = pltpu.roll(a, 16 * k, axis=1) if k else a
            kept = jnp.where((lane >> 4) == sub, turned, 0.0)
            out = out + (pltpu.roll(kept, 8 - k, axis=0) if k else kept)
        return out

    def stage_one(block):
        rows[0] = block
        rows[1, pl.ds(g, 1)] = rows[0, pl.ds(g, 1)]
        copies = []
        for k in range(1, NG):
            o = ((g + k) & (NG - 1))
            c = pltpu.make_async_remote_copy(
                src_ref=rows.at[0, pl.ds(o, 1)], dst_ref=rows.at[1, pl.ds(g, 1)],
                send_sem=g_send.at[k], recv_sem=g_recv.at[k],
                device_id=(o, b), device_id_type=MESH)
            c.start()
            copies.append(c)
        return copies

    def stage_two(first):
        for c in first:
            c.wait_recv()
        copies = []
        for k in range(1, NB):
            c = pltpu.make_async_remote_copy(
                src_ref=rows.at[1], dst_ref=gath.at[b],
                send_sem=b_send.at[k], recv_sem=b_recv.at[k],
                device_id=(g, ((b + k) & (NB - 1))), device_id_type=MESH)
            c.start()
            copies.append(c)
        gath[b] = rows[1]
        return copies

    def finish(second):
        for c in second:
            c.wait_recv()
        lane = iota((8, 128), 1)
        out = jnp.zeros((8, 128), jnp.float32)
        for k in range(NB):
            turned = pltpu.roll(gath[k], lax.rem(k - b + 128, 128), axis=1)
            out = out + jnp.where((lane & 15) == k, turned, 0.0)
        return swap(out)

    def post(n, block):
        pad = jnp.zeros((128 - block.shape[0], 128), jnp.float32)
        outbox[n] = jnp.concatenate([block, pad], axis=0).T

        def act(tg, tb):
            pltpu.make_async_remote_copy(
                src_ref=outbox.at[n, pl.ds(tg * NB + tb, 1)], dst_ref=inbox.at[n, pl.ds(me, 1)],
                send_sem=a_send.at[n], recv_sem=a_recv.at[n],
                device_id=(tg, tb), device_id_type=MESH).start()
        each_other(act)
        inbox[n, pl.ds(me, 1)] = outbox[n, pl.ds(me, 1)]

    def everything(n):
        return pltpu.make_async_remote_copy(
            src_ref=outbox.at[n, pl.ds(0, NG * NB - 1)], dst_ref=inbox.at[n, pl.ds(0, NG * NB - 1)],
            send_sem=a_send.at[n], recv_sem=a_recv.at[n],
            device_id=(g, b), device_id_type=MESH)

    def collect(n, count):
        everything(n).wait_recv()
        return inbox[n].T[0:count]

    def make_hot(hot, low):
        for q in range(8):
            hit = iota((128, 128), 0) == low[q:q + 1, :]
            hot[:, q * 128:(q + 1) * 128] = jnp.where(hit, 1.0, 0.0).astype(jnp.bfloat16)

    def lookup(parts, hot, high, count):
        stacked = jnp.concatenate(parts, axis=0)
        found = jnp.dot(stacked, hot[...], preferred_element_type=jnp.float32)
        total = found[:count] + found[count:2 * count] + found[2 * count:]
        out = []
        for q in range(8):
            piece = total[:, q * 128:(q + 1) * 128]
            hit = iota((count, 128), 0) == high[q:q + 1, :]
            out.append(jnp.sum(jnp.where(hit, piece, 0.0), axis=0, keepdims=True))
        return jnp.concatenate(out, axis=0)

    def scatter(values, hot, high, count):
        spread = jnp.concatenate(
            [jnp.where(iota((count, 128), 0) == high[q:q + 1, :], values[q:q + 1, :], 0.0)
             for q in range(8)], axis=1)
        total = jnp.zeros((count, 128), jnp.float32)
        for part in split3(spread):
            total = total + lax.dot_general(
                part, hot[...], (((1,), (1,)), ((), ())), preferred_element_type=jnp.float32)
        return total

    def zero_edges():
        for edge, plane, side in ((g == 0, 0, None), (g == NG - 1, CX + 1, None),
                                  (b == 0, None, 0), (b == NB - 1, None, 1)):
            @pl.when(edge)
            def _():
                for f in range(7):
                    if plane is not None:
                        fld[f, plane] = jnp.zeros((CY, CZ), jnp.float32)
                    else:
                        yrecv[f, side] = jnp.zeros((CX, CZ), jnp.float32)

    def faces(f):
        def remote(src, dst, way, target):
            return pltpu.make_async_remote_copy(
                src_ref=src, dst_ref=dst, send_sem=xs_sem.at[f, way], recv_sem=xr_sem.at[f, way],
                device_id=target, device_id_type=MESH)
        return (
            (g > 0, g < NG - 1, remote(fld.at[f, 1], fld.at[f, CX + 1], 0, (lax.max(g - 1, 0), b))),
            (g < NG - 1, g > 0, remote(fld.at[f, CX], fld.at[f, 0], 1, (lax.min(g + 1, NG - 1), b))),
            (b > 0, b < NB - 1, remote(ysend.at[f, 0], yrecv.at[f, 1], 2, (g, lax.max(b - 1, 0)))),
            (b < NB - 1, b > 0, remote(ysend.at[f, 1], yrecv.at[f, 0], 3, (g, lax.min(b + 1, NB - 1)))),
        )

    def send(f):
        for sends, _, c in faces(f):
            @pl.when(sends)
            def _():
                c.start()

    def arrive(f):
        for _, receives, c in faces(f):
            @pl.when(receives)
            def _():
                c.wait_recv()

    def sent(f):
        for sends, _, c in faces(f):
            @pl.when(sends)
            def _():
                c.wait_send()

    row = iota((CY, CZ), 0)
    col = iota((CY, CZ), 1)

    def y_down(a):
        return pltpu.roll(a, 1, axis=0)

    def y_up(a):
        return pltpu.roll(a, CY - 1, axis=0)

    def k_down(a):
        return pltpu.roll(a, 1, axis=1)

    def k_up(a):
        return pltpu.roll(a, CZ - 1, axis=1)

    def planes(step, carry):
        carry = lax.fori_loop(1, CX - 3, lambda x, c: step(x, c, False), carry, unroll=4)
        for x in range(CX - 3, CX + 1):
            carry = step(x, carry, x == CX)

    def conduct(n, f):
        def body(x, _):
            h = jnp.tanh(fld[f, x])
            d = fld[DD, x] * HALF_RATE
            kay[n, x] = d + (0.5 * d) * h
            slp[n, x] = (0.5 * d) * (1.0 - h * h)
            return 0
        lax.fori_loop(1, CX + 1, body, 0, unroll=4)

    def conduct_own(n, f):
        for side in range(2):
            h = jnp.tanh(ysend[f, side])
            d = ysend[DD, side] * HALF_RATE
            kyf[n, side] = d + (0.5 * d) * h
            syf[n, side] = (0.5 * d) * (1.0 - h * h)

    def conduct_halo(n, f):
        for x in (0, CX + 1):
            kay[n, x] = HALF_RATE * fld[DD, x] * (1.0 + 0.5 * jnp.tanh(fld[f, x]))
        for side in range(2):
            kyh[n, side] = HALF_RATE * yrecv[DD, side] * (1.0 + 0.5 * jnp.tanh(yrecv[f, side]))

    def forward(n, f, out):
        def step(x, flow_low, last):
            t, k = fld[f, x], kay[n, x]
            acc = (1.0 - DRIFT) * t - flow_low[0] + flow_low[1]
            flow = None
            if not last:
                flow = (k + kay[n, x + 1]) * (fld[f, x + 1] - t)
                acc = acc + flow
            y_l = jnp.where(row == 0, 0.0, (k + y_down(k)) * (t - y_down(t)))
            acc = acc + (y_up(y_l) - y_l)
            kt = k * t
            k_l = jnp.where(col == 0, kt, (k + k_down(k)) * (t - k_down(t)))
            acc = acc + (jnp.where(col == CZ - 1, -kt, k_up(k_l)) - k_l)
            fld[out, x] = acc
            return flow, DRIFT * t
        zero = jnp.zeros((CY, CZ), jnp.float32)
        planes(step, (zero, zero))

    def forward_faces(n, f, out):
        low, high = fld[f, 0], fld[f, CX + 1]
        fld[out, 1] = fld[out, 1] + DRIFT * low - (kay[n, 0] + kay[n, 1]) * (fld[f, 1] - low)
        fld[out, CX] = fld[out, CX] + (kay[n, CX] + kay[n, CX + 1]) * (high - fld[f, CX])
        for side in range(2):
            delta[side] = (kyf[n, side] + kyh[n, side]) * (yrecv[f, side] - ysend[f, side])

    def reverse(n, f, lam, out):
        def step(x, carry, last):
            g_x, m_x = carry
            t, k, l = fld[f, x], kay[n, x], fld[lam, x]
            bend = g_x
            acc = (1.0 - DRIFT) * l + m_x
            g_u = m_u = None
            if not last:
                l_up = fld[lam, x + 1]
                w = l - l_up
                g_u = w * (fld[f, x + 1] - t)
                m_u = w * (k + kay[n, x + 1])
                bend = bend + g_u
                acc = acc + (DRIFT * l_up - m_u)
            w = jnp.where(row == 0, 0.0, y_down(l) - l)
            g_l = w * (t - y_down(t))
            m_l = w * (k + y_down(k))
            bend = bend + (g_l + y_up(g_l))
            acc = acc + (m_l - y_up(m_l))
            lt, lk = l * t, l * k
            w = k_down(l) - l
            g_l = jnp.where(col == 0, -lt, w * (t - k_down(t)))
            m_l = jnp.where(col == 0, -lk, w * (k + k_down(k)))
            bend = bend + (g_l + jnp.where(col == CZ - 1, -lt, k_up(g_l)))
            acc = acc + (m_l - jnp.where(col == CZ - 1, lk, k_up(m_l)))
            value = acc + slp[n, x] * bend
            if out is None:
                adj_ref[x - 1] = value
            else:
                fld[out, x] = value
            return g_u, m_u
        zero = jnp.zeros((CY, CZ), jnp.float32)
        planes(step, (zero, zero))

    def reverse_faces(n, f, lam, out):
        w = fld[lam, 0] - fld[lam, 1]
        low = (slp[n, 1] * (w * (fld[f, 1] - fld[f, 0])) + w * (kay[n, 0] + kay[n, 1]))
        w = fld[lam, CX] - fld[lam, CX + 1]
        high = (slp[n, CX] * (w * (fld[f, CX + 1] - fld[f, CX])) - w * (kay[n, CX] + kay[n, CX + 1])
                + DRIFT * fld[lam, CX + 1])
        if out is None:
            adj_ref[0] = adj_ref[0] + low
            adj_ref[CX - 1] = adj_ref[CX - 1] + high
        else:
            fld[out, 1] = fld[out, 1] + low
            fld[out, CX] = fld[out, CX] + high
        for side in range(2):
            w = yrecv[lam, side] - ysend[lam, side]
            bend = w * (ysend[f, side] - yrecv[f, side])
            delta[side] = syf[n, side] * bend + w * (kyf[n, side] + kyh[n, side])

    def add_delta(f):
        def body(x, _):
            for side, y in ((0, slice(0, 1)), (1, slice(CY - 1, CY))):
                if f is None:
                    adj_ref[x, y] = adj_ref[x, y] + delta[side, pl.ds(x, 1), :]
                else:
                    new = fld[f, x + 1, y] + delta[side, pl.ds(x, 1), :]
                    fld[f, x + 1, y] = new
                    ysend[f, side, pl.ds(x, 1), :] = new
            return 0
        lax.fori_loop(0, CX, body, 0, unroll=4)

    wide = iota((TR, 128), 1)
    tall = iota((TR, 128), 0)
    strip = (tall * 1366) >> 16
    inside = tall - WY * strip
    outside = (
        ((strip == 0) & (g == 0)) | ((strip == 5) & (g == NG - 1))
        | ((inside < 8) & (b == 0)) | ((inside >= 8 + CY) & (b == NB - 1))
    )
    surface = (wide & 15) == 0

    def in_grid(a):
        return jnp.where(outside, 0.0, a)

    def next_x(a):
        r = pltpu.roll(a, 112, axis=1)
        return jnp.where(wide < 112, r, jnp.concatenate([r[WY:], r[:WY]], axis=0))

    def last_x(a):
        r = pltpu.roll(a, 16, axis=1)
        return jnp.where(wide >= 16, r, jnp.concatenate([r[TR - WY:], r[:TR - WY]], axis=0))

    def next_y(a):
        return pltpu.roll(a, TR - 1, axis=0)

    def last_y(a):
        return pltpu.roll(a, 1, axis=0)

    def next_k(a):
        return pltpu.roll(a, 127, axis=1)

    def last_k(a):
        return pltpu.roll(a, 1, axis=1)

    def top_conduct(t, d):
        h = jnp.tanh(t)
        d = d * HALF_RATE
        return d + (0.5 * d) * h, (0.5 * d) * (1.0 - h * h)

    def top_forward(t, k):
        flow = (k + next_x(k)) * (next_x(t) - t)
        acc = (1.0 - DRIFT) * t + DRIFT * last_x(t) + (flow - last_x(flow))
        flow = (k + next_y(k)) * (next_y(t) - t)
        acc = acc + (flow - last_y(flow))
        flow = jnp.where(surface, k * t, (k + last_k(k)) * (t - last_k(t)))
        return acc + (next_k(flow) - flow)

    def top_reverse(t, k, s, l):
        l_up = next_x(l)
        w = l - l_up
        bent = w * (next_x(t) - t)
        moved = w * (k + next_x(k))
        bend = bent + last_x(bent)
        acc = (1.0 - DRIFT) * l + DRIFT * l_up + (last_x(moved) - moved)
        w = l - next_y(l)
        bent = w * (next_y(t) - t)
        moved = w * (k + next_y(k))
        bend = bend + (bent + last_y(bent))
        acc = acc + (last_y(moved) - moved)
        w = last_k(l) - l
        bent = jnp.where(surface, -(l * t), w * (t - last_k(t)))
        moved = jnp.where(surface, -(l * k), w * (k + last_k(k)))
        bend = bend + (bent + next_k(bent))
        acc = acc + (moved - next_k(moved))
        return in_grid(acc + s * bend)

    def top_pack():
        lane = iota((CY, 128), 1) >> 4
        for i, f in enumerate((T0, DD, L3)):
            for strip_x in range(4):
                x = 1 + 8 * strip_x
                tile = fld[f, x, :, 0:128]
                for j in range(1, 8):
                    tile = jnp.where(lane == j, pltpu.roll(fld[f, x + j, :, 0:128], 16 * j, axis=1), tile)
                top[i, 1 + strip_x, 8:8 + CY] = tile
        entry = jnp.concatenate([entry_ref[...], jnp.zeros((CX, 128 - CY), jnp.int32)], axis=1)
        entry = jnp.concatenate([entry.astype(jnp.float32), jnp.zeros((128 - CX, 128), jnp.float32)], axis=0)
        entry = entry.T[0:CY].astype(jnp.int32)
        spread = jnp.where(iota((128, 512), 0) == (iota((128, 512), 1) >> 4), 1.0, 0.0).astype(jnp.bfloat16)
        high = jnp.dot((entry >> 3).astype(jnp.float32).astype(jnp.bfloat16), spread,
                       preferred_element_type=jnp.float32)
        low = jnp.dot((entry & 7).astype(jnp.float32).astype(jnp.bfloat16), spread,
                      preferred_element_type=jnp.float32)
        entry = 8.0 * high + low
        for strip_x in range(4):
            top[3, 1 + strip_x, 8:8 + CY] = entry[:, 128 * strip_x:128 * (strip_x + 1)]

    def top_copies():
        out = []
        along_x = {-1: (1, 1, 5), 0: (1, 4, 1), 1: (4, 1, 0)}
        along_y = {-1: (8, 8, 8 + CY), 0: (8, CY, 8), 1: (CY, 8, 0)}
        for dx in (-1, 0, 1):
            for dy in (-1, 0, 1):
                if dx == 0 and dy == 0:
                    continue
                way = (dx + 1) * 3 + dy + 1
                x, wide_x, to_x = along_x[dx]
                y, wide_y, to_y = along_y[dy]
                sends, receives = None, None
                for d, at, size in ((dx, g, NG), (dy, b, NB)):
                    if d:
                        one = (at > 0, at < size - 1)
                        one = one if d < 0 else one[::-1]
                        sends = one[0] if sends is None else sends & one[0]
                        receives = one[1] if receives is None else receives & one[1]
                target = (lax.clamp(0, g + dx, NG - 1), lax.clamp(0, b + dy, NB - 1))
                out.append((sends, receives, pltpu.make_async_remote_copy(
                    src_ref=top.at[:, pl.ds(x, wide_x), pl.ds(y, wide_y)],
                    dst_ref=top.at[:, pl.ds(to_x, wide_x), pl.ds(to_y, wide_y)],
                    send_sem=t_send.at[way], recv_sem=t_recv.at[way],
                    device_id=target, device_id_type=MESH)))
        return out

    def when(condition, action):
        @pl.when(condition)
        def _():
            action()

    line = iota((1, TL), 1)
    line_strip = (line * 1366) >> 16
    line_y = line - WY * line_strip
    side_x = jnp.where(line_strip == 0, 0, jnp.where(line_strip >= 5, 2, 1))
    side_y = jnp.where(line_y < 8, 0, jnp.where(line_y >= 8 + CY, 2, 1))
    whose = 3 * side_x + side_y
    ours = whose == 4

    def to_lines(a):
        turned = jnp.concatenate([a, jnp.zeros((TL - TR, 128), jnp.float32)], axis=0).T
        return jnp.concatenate([turned[16 * j:16 * j + 1] for j in range(8)], axis=0)

    def from_lines(lines):
        turn[...] = jnp.zeros((128, TL), jnp.float32)
        for j in range(8):
            turn[16 * j:16 * j + 1, :] = lines[j]
        return turn[...].T[0:TR]

    def neighbours(v):
        return jnp.concatenate(
            [pltpu.roll(v, (-(NB * dx + dy)) % 128, axis=1) if dx or dy else v
             for dx in (-1, 0, 1) for dy in (-1, 0, 1)], axis=0)

    def top_hot(entry):
        for j in range(8):
            hit = iota((128, TL), 0) == (entry[j:j + 1] >> 3)
            hot_n[:, j * TL:(j + 1) * TL] = jnp.where(hit, 1.0, 0.0).astype(jnp.bfloat16)

    def top_heat(slots, entry):
        stacked = jnp.concatenate(split3(slots), axis=0)
        lines = []
        for j in range(8):
            found = jnp.dot(stacked, hot_n[:, j * TL:(j + 1) * TL], preferred_element_type=jnp.float32)
            found = found[:72] + found[72:144] + found[144:]
            hit = iota((72, TL), 0) == 8 * whose + (entry[j:j + 1] & 7)
            lines.append(jnp.sum(jnp.where(hit, found, 0.0), axis=0, keepdims=True))
        return from_lines(lines)

    def top_slots(a, entry):
        lines = to_lines(a)
        spread = jnp.concatenate(
            [jnp.where((iota((8, TL), 0) == (entry[j:j + 1] & 7)) & ours, lines[j:j + 1], 0.0)
             for j in range(8)], axis=1)
        stacked = jnp.concatenate(split3(spread), axis=0)
        total = lax.dot_general(
            stacked, hot_n[...], (((1,), (1,)), ((), ())), preferred_element_type=jnp.float32)
        return total[0:8] + total[8:16] + total[16:24]

    def overlay():
        lane = iota((CY, 128), 1)
        for x in range(CX):
            rows = nst[LAM0, (1 + x // 8) * WY + 8:(1 + x // 8) * WY + 8 + CY]
            j = x % 8
            rows = pltpu.roll(rows, 128 - 16 * j, axis=1) if j else rows
            adj_ref[x, :, 0:128] = jnp.where(lane < 5, rows, adj_ref[x, :, 0:128])

    zero_edges()
    table = swap(table_ref[...].astype(jnp.float32))
    pl.semaphore_wait(barrier, NG - 1 + NB - 1 + len(corners))
    first = stage_one(table)
    for i, f in ((0, T0), (1, DD), (2, L3)):
        for load in edge_loads[i]:
            load.wait()
        loads[i].wait()
        if f != L3:
            send(f)
    conduct(0, T0)
    conduct_own(0, T0)
    top_pack()
    tops = top_copies()
    send(L3)
    forward(0, T0, T1)
    second = stage_two(first)
    arrive(T0)
    arrive(DD)
    conduct_halo(0, T0)
    forward_faces(0, T0, T1)
    add_delta(T1)
    send(T1)
    for sends, _, c in tops:
        when(sends, c.start)
    patches = split3(patch_ref[...])

    spot = finish(second).astype(jnp.int32)
    p_high = spot >> 7
    make_hot(hot_p, spot & 127)
    post(0, neighbours(lookup(patches, hot_p, p_high, 64)))

    conduct(1, T1)
    conduct_own(1, T1)
    forward(1, T1, T2)

    arrive(T1)
    conduct_halo(1, T1)
    forward_faces(1, T1, T2)
    add_delta(T2)
    send(T2)

    for _, receives, c in tops:
        when(receives, c.wait_recv)
    def whole(i):
        return top[i].reshape(TR, 128)
    t0, d, l3 = in_grid(whole(0)), in_grid(whole(1)), in_grid(whole(2))
    entry = to_lines(whole(3)).astype(jnp.int32)
    top_hot(entry)
    k0, s0 = top_conduct(t0, d)
    nst[KAY0], nst[SLP0] = k0, s0
    nst[TEM1] = top_forward(t0, k0)

    conduct(2, T2)
    conduct_own(2, T2)
    reverse(2, T2, L3, L2)
    arrive(L3)
    arrive(T2)
    conduct_halo(2, T2)
    reverse_faces(2, T2, L3, L2)
    add_delta(L2)
    send(L2)
    heat = SOURCE * top_heat(collect(0, 72), entry)
    t1 = in_grid(nst[TEM1] + heat)
    k1, s1 = top_conduct(t1, d)
    t2 = in_grid(top_forward(t1, k1) + heat)
    k2, s2 = top_conduct(t2, d)
    l2 = top_reverse(t2, k2, s2, l3)
    l1 = top_reverse(t1, k1, s1, l2)
    post(1, top_slots(SOURCE * (l3 + l2 + l1), entry))
    nst[LAM1] = l1

    reverse(1, T1, L2, L1)
    arrive(L2)
    reverse_faces(1, T1, L2, L1)
    add_delta(L1)
    send(L1)
    nst[LAM0] = top_reverse(in_grid(whole(0)), nst[KAY0], nst[SLP0], nst[LAM1])
    reverse(0, T0, L1, None)
    flux_ref[...] = scatter(collect(1, 8), hot_p, p_high, 64)
    arrive(L1)
    reverse_faces(0, T0, L1, None)
    add_delta(None)
    overlay()

    for n in range(2):
        everything(n).wait_send()
    for c in first + second:
        c.wait_send()
    for f in range(7):
        sent(f)
    for sends, _, c in tops:
        when(sends, c.wait_send)


def shards(state, diffusivity, patches, entries, table, sensitivity):
    anywhere = pl.BlockSpec(memory_space=pl.ANY)
    vmem = pl.BlockSpec(memory_space=pltpu.VMEM)
    f32, bf16 = jnp.float32, jnp.bfloat16
    flux, adjoint = pl.pallas_call(
        kernel,
        out_shape=(
            jax.ShapeDtypeStruct((64, 128), f32),
            jax.ShapeDtypeStruct((CX, CY, CZ), f32),
        ),
        in_specs=[anywhere, anywhere, anywhere, vmem, vmem, vmem],
        out_specs=(vmem, vmem),
        scratch_shapes=[
            pltpu.VMEM((7, CX + 2, CY, CZ), f32),
            pltpu.VMEM((3, CX + 2, CY, CZ), f32),
            pltpu.VMEM((3, CX + 2, CY, CZ), f32),
            pltpu.VMEM((7, 2, CX, CZ), f32),
            pltpu.VMEM((7, 2, CX, CZ), f32),
            pltpu.VMEM((3, 2, CX, CZ), f32),
            pltpu.VMEM((3, 2, CX, CZ), f32),
            pltpu.VMEM((3, 2, CX, CZ), f32),
            pltpu.VMEM((2, CX, CZ), f32),
            pltpu.VMEM((2, NG * NB, 128), f32),
            pltpu.VMEM((2, NG * NB, 128), f32),
            pltpu.VMEM((2, 8, 128), f32),
            pltpu.VMEM((NB, 8, 128), f32),
            pltpu.VMEM((128, 8 * TL), bf16),
            pltpu.VMEM((128, 1024), bf16),
            pltpu.VMEM((4, 6, WY, 128), f32),
            pltpu.VMEM((5, TR, 128), f32),
            pltpu.VMEM((128, TL), f32),
            pltpu.SemaphoreType.DMA((3, 3)),
            pltpu.SemaphoreType.DMA((7, 4)),
            pltpu.SemaphoreType.DMA((7, 4)),
            pltpu.SemaphoreType.DMA((3,)),
            pltpu.SemaphoreType.DMA((3,)),
            pltpu.SemaphoreType.DMA((NG,)),
            pltpu.SemaphoreType.DMA((NG,)),
            pltpu.SemaphoreType.DMA((NB,)),
            pltpu.SemaphoreType.DMA((NB,)),
            pltpu.SemaphoreType.DMA((9,)),
            pltpu.SemaphoreType.DMA((9,)),
        ],
        compiler_params=pltpu.CompilerParams(
            collective_id=0, has_side_effects=True, vmem_limit_bytes=52 * 1024 * 1024),
    )(
        state, diffusivity, sensitivity, patches.reshape(64, 128),
        entries, jnp.swapaxes(table[0], 0, 1),
    )
    return flux.reshape(-1), adjoint


def solution(mesh):
    return jax.shard_map(
        shards,
        mesh=mesh,
        in_specs=(
            P("gx", "bulk", None),
            P("gx", "bulk", None),
            P(("gx", "bulk")),
            P("gx", "bulk"),
            P(("gx", "bulk"), None, None),
            P("gx", "bulk", None),
        ),
        out_specs=(P(("gx", "bulk")), P("gx", "bulk", None)),
        check_vma=False,
    )
```
